32 devices in a mesh: tok: 4 (over y, core), exp: 8 (over z, x).
Axes of the slice: x: 2, y: 2, z: 4, core: 2. Of those that a mesh axis runs over, the one named last changes fastest.
Arguments:
- x_tokens: bfloat16 [4096, 4096], P(('tok', 'exp')), may hold values from -48 to 48
- router_weight: bfloat16 [4096, 512], replicated, may hold values from -1 to 1
- gate_rest: float32 [4096, 508], P(('tok', 'exp')), may hold values from -192 to 192
- latent_in: bfloat16 [4096, 1024], P(('tok', 'exp')), may hold values from -6 to 6
- latent_grad: bfloat16 [4096, 1024], P(('tok', 'exp')), may hold values from -6 to 6
- expert_picks: int32 [4096, 22], P('tok'), may hold values from 0 to 511, all different within a row; in each aligned block of 128 rows (0 to 127, 128 to 255, ...) at most 12 rows name the same one
- expert_in: bfloat16 [8, 1024, 1344], P('exp'), may hold values from -0.1875 to 0.1875
- expert_out: bfloat16 [8, 1344, 1024], P('exp'), may hold values from -0.125 to 0.125
Outputs:
- latent_in_grad: bfloat16 [4096, 1024], P(('tok', 'exp'))
- x_grad: bfloat16 [4096, 4096], P(('tok', 'exp'))
- router_weight_grad: float32 [4096, 512], P(('tok', 'exp'))
The draws below stay inside these ranges and needn't reach their ends.
Inputs may be any that keep to these rules, and one draw needn't show every extreme that they name: `expert_picks`: each row names 22 different experts. Within each aligned block of 128 rows (the rows of one device) no expert is named more than 12 times, a bound that some block reaches; every expert is named somewhere.
All inputs are finite; a program needn't handle non-finite values.
Results may differ from the reference program's by a relative error of at most 0.009.
Values may be sent and summed in bfloat16 or wider, within the bound.
A program may use at most 128 MiB of HBM per device.

```python
import math
import jax
import jax.numpy as jnp
import numpy as np
from jax import lax

D = 4096
L = 1024
H = 2688
EXPERTS = 512
TOP = 22
TOK_DEV = 128
TOKENS = 4096
WIN = 4
HB = 1344
BLOCKS = 8
SLOT_DEPTH = 12


def router_table(key):
    return jax.random.normal(jax.random.fold_in(key, 11), (D, EXPERTS), jnp.float32) * (0.5 / math.sqrt(D))


def draw_router_weight(key, part):
    return router_table(key).astype(jnp.bfloat16)


def draw_x_tokens(key, part):
    base = jnp.clip(jax.random.normal(jax.random.fold_in(key, 12), (TOKENS, D), jnp.float32), -6.0, 6.0)
    result = base
    return result.astype(jnp.bfloat16)


def shard_levels(rng, extent, pieces, least, high):
    gain = 1.0
    for axis_at, shards_of in pieces:
        heights = jax.random.uniform(jax.random.fold_in(jax.random.fold_in(rng, 6), axis_at), (shards_of,), jnp.float32, least / len(pieces), high / len(pieces))
        gain = gain * jnp.repeat(jnp.exp(heights), extent[axis_at] // shards_of).reshape((-1,) + (1,) * (len(extent) - 1 - axis_at))
    return gain


def routed_block(own_key, own, number, rows, number_of, top, most, lean):
    sequence = jax.random.permutation(own_key, number_of)
    heavy_load, ordinary = portions_of(number_of, rows * top, most, lean, True), portions_of(number_of, rows * top, most, lean, False)
    places = jnp.arange(number_of)

    def named(sizes, rotation):
        used = int((sizes > 0).sum())
        fixed = max(1, used // 4)
        shifted = fixed + (places - fixed + rotation * (used - fixed)) % max(1, number_of - fixed)
        return jnp.zeros((number_of,), jnp.int32).at[sequence[jnp.where(places < fixed, places, shifted)]].set(jnp.asarray(sizes, jnp.int32))

    sizes = jnp.where(number % 4 == 0, named(heavy_load, number // 4), named(ordinary, number - number // 4 - 1))
    mixed = jax.random.permutation(jax.random.fold_in(own, 3), number_of)
    source_of, taker = mixed[0:number_of // 2 * 2:2], mixed[1:number_of // 2 * 2:2]
    slack = jnp.minimum(sizes[source_of] - 1, most - sizes[taker]) // 2
    slack = jnp.where((source_of == sequence[0]) | (taker == sequence[0]) | (sizes[taker] == 0), 0, jnp.maximum(slack, 0))
    shifted = jax.random.randint(jax.random.fold_in(own, 4), (number_of // 2,), 0, 1 << 20) % (slack + 1)
    sizes = sizes.at[source_of].add(-shifted).at[taker].add(shifted)
    items = jnp.searchsorted(jnp.cumsum(sizes), jnp.arange(rows * top), side="right").astype(jnp.int32)
    table = items.reshape(top, rows).T
    table = table[jax.random.permutation(jax.random.fold_in(own, 1), rows)]
    rotation = jax.random.randint(jax.random.fold_in(own, 2), (rows, 1), 0, top)
    return jnp.take_along_axis(table, (jnp.arange(top)[None, :] + rotation) % top, axis=1)


def portions_of(count, total, most, lean, full):
    portions = [(1 << 20) // math.isqrt(standing ** lean) + 1 for standing in range(1, count + 1)]
    largest = most if full else min(most, max(-(-total // count), total * portions[0] // sum(portions)))
    least = 1 if total - largest >= count - 1 else 0
    holding, surplus = [largest] + [least] * (count - 1), total - largest - least * (count - 1)
    while surplus > 0:
        movable = [i for i in range(1, count) if holding[i] < largest] or [i for i in range(1, count) if holding[i] < most]
        mass, left = sum([portions[i] for i in movable]), surplus
        for i in movable:
            more = min(most - holding[i], max(1, left * portions[i] // mass), surplus)
            holding[i] = holding[i] + more
            surplus = surplus - more
    return np.array(holding)


def gaussian(key, extent, deviation, reach, split=(), held_as=jnp.bfloat16):
    entries = deviation * jax.random.normal(key, extent, jnp.float32)
    if split:
        entries = entries * shard_levels(key, extent, split, -0.22, 0.18)
    return jnp.clip(entries, -reach, reach).astype(held_as)


def setup_inputs(seed: int = 0) -> dict:
    seeds = jax.random.split(jax.random.key(seed), 9)
    x_tokens = draw_x_tokens(jax.random.fold_in(seeds[8], 71), 0)
    router_weight = draw_router_weight(jax.random.fold_in(seeds[8], 71), 0)
    gate_rest = gaussian(seeds[2], (TOKENS, EXPERTS - WIN), 32.0, 192.0, ((0, 32),), jnp.float32)
    latent_in = gaussian(seeds[3], (TOKENS, L), 1.0, 6.0, ((0, 32),))
    latent_grad = gaussian(seeds[4], (TOKENS, L), 1.0, 6.0, ((0, 32),))
    expert_picks_keys = jax.random.split(jax.random.fold_in(seeds[5], 1), TOKENS // TOK_DEV)
    expert_picks_turns = jax.random.permutation(jax.random.fold_in(seeds[5], 3), TOKENS // TOK_DEV)
    expert_picks = jax.vmap(lambda own, number: routed_block(jax.random.fold_in(seeds[5], 2), own, number, TOK_DEV, EXPERTS, TOP, SLOT_DEPTH, 2))(expert_picks_keys, expert_picks_turns).reshape((TOKENS, TOP))
    expert_in = gaussian(seeds[6], (BLOCKS, L, HB), L ** -0.5, 0.1875, ((0, 8),))
    expert_out = gaussian(seeds[7], (BLOCKS, HB, L), H ** -0.5, 0.125, ((0, 8),))
    return {"x_tokens": x_tokens, "router_weight": router_weight, "gate_rest": gate_rest, "latent_in": latent_in, "latent_grad": latent_grad, "expert_picks": expert_picks, "expert_in": expert_in, "expert_out": expert_out}


def reference(x_tokens, router_weight, gate_rest, latent_in, latent_grad, expert_picks, expert_in, expert_out):
    logits = jnp.dot(x_tokens, router_weight, preferred_element_type=jnp.float32)
    probs = jax.nn.softmax(logits, axis=-1)
    window_ids = jnp.arange(WIN, dtype=jnp.int32)
    chosen = jnp.any(expert_picks[:, :, None] == window_ids[None, None, :], axis=1)
    picked_probs = jnp.where(chosen, probs[:, :WIN], jnp.float32(0.0))
    full_in = jnp.transpose(expert_in.reshape(WIN, 2, L, HB), (0, 2, 1, 3)).reshape(WIN, L, H)
    full_out = expert_out.reshape(WIN, H, L)

    def one_expert(running, item):
        weight_a, weight_b, column = item
        preact = jnp.dot(latent_in, weight_a, preferred_element_type=jnp.float32)
        hidden_grad = jnp.dot(latent_grad, weight_b.T, preferred_element_type=jnp.float32)
        active = jnp.maximum(preact, 0.0)
        gate_column = jnp.sum(active * active * hidden_grad, axis=1)
        coeff = (column[:, None] * 2.0 * active * hidden_grad).astype(jnp.bfloat16)
        running = running + jnp.dot(coeff, weight_a.T, preferred_element_type=jnp.float32)
        return running, gate_column

    initial = jnp.zeros((TOKENS, L), jnp.float32)
    latent_sum, gate_columns = lax.scan(one_expert, initial, (full_in, full_out, picked_probs.T))
    gate_grad = jnp.concatenate([gate_columns.T, gate_rest], axis=1)
    centre = jnp.sum(probs * gate_grad, axis=-1, keepdims=True)
    logit_grad = probs * (gate_grad - centre)
    logit_low = logit_grad.astype(jnp.bfloat16)
    x_grad = jnp.dot(logit_low, router_weight.T, preferred_element_type=jnp.float32).astype(jnp.bfloat16)
    router_weight_grad = jnp.dot(x_tokens.T, logit_low, preferred_element_type=jnp.float32)
    return latent_sum.astype(jnp.bfloat16), x_grad, router_weight_grad
```

```python
import functools
import jax
import jax.numpy as jnp
from jax import lax
from jax.experimental import pallas as pl
from jax.experimental.pallas import tpu as pltpu
from jax.sharding import PartitionSpec as P

MESH = pl.DeviceIdType.MESH
F32 = jnp.float32
BF16 = jnp.bfloat16
NT = (((1,), (1,)), ((), ()))
SLOTS = 16


def kernel(
    toks, lanes, window,
    x_ref, gate_ref, latin_ref, latgrad_ref, hits_ref, own_hits_ref, rw_hbm, win_hbm, wout_hbm,
    latent_out, xgrad_out, rwg_out,
    rw, win, wout, lat, probs, pick_recv, pick_send, gate_recv, gate_send, gate_rows, rank, packed,
    term_send, term_recv, xband, xturned, logits_all, part_mine, part_send, part_recv,
    zpart_send, zpart_recv,
    load_sem, send_lat, recv_z, recv_x, pick_ss, pick_rs, gate_ss, gate_rs, term_ss, term_rs,
    band_ss, band_rs, log_ss, log_rs, px_ss, px_rs, pz_ss, pz_rs,
):
    tok = lax.axis_index("tok")
    lane = lax.axis_index("exp")
    outers = lanes // 2
    outer = lane // 2
    inner = lane % 2
    expert = lane // 2
    rows = x_ref.shape[0]
    feats = x_ref.shape[1] // toks
    own_rows = feats // lanes

    loads = [
        pltpu.make_async_copy(rw_hbm, rw, load_sem.at[0]),
        pltpu.make_async_copy(win_hbm.at[0], win, load_sem.at[1]),
        pltpu.make_async_copy(wout_hbm.at[0], wout, load_sem.at[2]),
    ]
    for load in loads:
        load.start()

    def at_lane(k):
        return lax.rem(lane + k, lanes)

    def at_tok(k):
        return lax.rem(tok + k, toks)

    barrier = pltpu.get_barrier_semaphore()
    for k in range(1, lanes):
        pl.semaphore_signal(barrier, inc=1, device_id={"exp": at_lane(k)}, device_id_type=MESH)
    for k in range(1, toks):
        pl.semaphore_signal(barrier, inc=1, device_id={"tok": at_tok(k)}, device_id_type=MESH)
    lat[0, lane] = latin_ref[...]
    lat[1, lane] = latgrad_ref[...]
    pl.semaphore_wait(barrier, lanes - 1 + toks - 1)

    def lat_copy(kind, which, src_outer, src_inner):
        slot = src_outer * 2 + src_inner
        if kind == 2:
            peer, recv = outer * 2 + 1 - inner, recv_x.at[which, src_outer]
        else:
            peer, recv = lane + (2 if kind == 0 else -2), recv_z.at[which, src_outer]
        return pltpu.make_async_remote_copy(
            src_ref=lat.at[which, slot], dst_ref=lat.at[which, slot],
            send_sem=send_lat.at[kind, which, src_outer], recv_sem=recv,
            device_id={"exp": peer}, device_id_type=MESH,
        )

    def forward(which, src_outer, do):
        @pl.when((src_outer <= outer) & (outer < outers - 1))
        def _():
            do(lat_copy(0, which, src_outer, inner))

        @pl.when((src_outer >= outer) & (outer > 0))
        def _():
            do(lat_copy(1, which, src_outer, inner))

        do(lat_copy(2, which, src_outer, inner))

    for which in range(2):
        forward(which, outer, lambda c: c.start())

    def band_copy(k):
        peer = at_tok(k)
        return pltpu.make_async_remote_copy(
            src_ref=x_ref.at[:, pl.ds(pl.multiple_of(peer * feats, 128), feats)],
            dst_ref=xband.at[toks - k],
            send_sem=band_ss.at[k], recv_sem=band_rs.at[toks - k],
            device_id={"tok": peer}, device_id_type=MESH,
        )

    for k in range(1, toks):
        band_copy(k).start()
    xband[0] = x_ref[:, pl.ds(pl.multiple_of(tok * feats, 128), feats)]

    loads[0].wait()
    logits = jnp.dot(x_ref[...], rw[...], preferred_element_type=F32)
    shifted = jnp.exp(logits - jnp.max(logits, axis=1, keepdims=True))
    probs[...] = shifted / jnp.sum(shifted, axis=1, keepdims=True)
    pad = own_hits_ref.shape[0]
    pick_send[...] = jnp.transpose(probs[:, :128])[:pad] * own_hits_ref[...]
    pick_recv[0] = pick_send[...]

    def pick_copy(k):
        return pltpu.make_async_remote_copy(
            src_ref=pick_send, dst_ref=pick_recv.at[lanes - k],
            send_sem=pick_ss.at[k], recv_sem=pick_rs.at[lanes - k],
            device_id={"exp": at_lane(k)}, device_id_type=MESH,
        )

    for k in range(1, lanes):
        pick_copy(k).start()
    before = (
        lax.broadcasted_iota(jnp.int32, (rows, rows), 0)
        <= lax.broadcasted_iota(jnp.int32, (rows, rows), 1)
    ).astype(BF16)
    rank[...] = jnp.dot(hits_ref[...].astype(BF16), before, preferred_element_type=F32) - 1.0
    slot_iota = lax.broadcasted_iota(jnp.int32, (SLOTS, rows), 0).astype(F32)
    loads[1].wait()
    loads[2].wait()
    for k in range(1, lanes):
        pick_copy(k).wait_recv()

    def gate_copy(src_lane):
        return pltpu.make_async_remote_copy(
            src_ref=gate_send.at[src_lane], dst_ref=gate_recv.at[lane],
            send_sem=gate_ss.at[src_lane], recv_sem=gate_rs.at[lane],
            device_id={"exp": src_lane}, device_id_type=MESH,
        )

    def expert_rows(src_lane):
        active = jnp.maximum(jnp.dot(lat[0, src_lane], win[...], preferred_element_type=F32), 0.0)
        grad = lax.dot_general(lat[1, src_lane], wout[...], NT, preferred_element_type=F32)
        product = active * grad
        gate = jnp.sum(active * product, axis=1, keepdims=True)
        gate_row = jnp.transpose(jnp.broadcast_to(gate, (rows, rows)))[:8]
        gate_send[src_lane] = gate_row

        @pl.when(src_lane == lane)
        def _():
            gate_recv[lane] = gate_row

        @pl.when(src_lane != lane)
        def _():
            gate_copy(src_lane).start()

        chosen = (
            (hits_ref[pl.ds(src_lane, 1), :] > 0.0) & (rank[pl.ds(src_lane, 1), :] == slot_iota)
        ).astype(F32)
        picked = pick_recv[lax.rem(src_lane - lane + lanes, lanes), pl.ds(expert, 1), :]
        scale = jnp.sum(chosen * picked, axis=1, keepdims=True)
        raw = jnp.dot(chosen.astype(BF16), (2.0 * product).astype(BF16), preferred_element_type=F32)
        packed[src_lane] = (raw * scale).astype(BF16)

    def arrivals(step, carry):
        for side in (-1, 1):
            src_outer = outer + side * step

            @pl.when((step > 0) & (step < outers) & (src_outer >= 0) & (src_outer < outers))
            def _():
                for which in range(2):
                    lat_copy(0, which, src_outer, inner).wait_recv()
                    forward(which, src_outer, lambda c: c.start())

        def piece(q, carry):
            across = q // 2
            side = q % 2
            distance = step - across
            src_outer = outer + (2 * side - 1) * distance
            valid = (src_outer >= 0) & (src_outer < outers) & (distance >= 0)
            valid = valid & ((distance > 0) | (side == 0)) & (distance < outers)

            @pl.when(valid & (across == 1))
            def _():
                for which in range(2):
                    lat_copy(2, which, src_outer, 1 - inner).wait_recv()

            @pl.when(valid)
            def _():
                expert_rows(src_outer * 2 + lax.rem(inner + across, 2))

            return carry

        lax.fori_loop(0, 4, piece, 0)

        @pl.when(step == outers - 1)
        def _():
            for k in range(toks):
                if k:
                    band_copy(k).wait_recv()
            for k in range(toks):
                xturned[:, k * rows:(k + 1) * rows] = jnp.transpose(xband[k])

        return carry

    lax.fori_loop(0, outers + 1, arrivals, 0)

    terms = lax.dot_general(
        packed[...].reshape(lanes * SLOTS, packed.shape[2]), win[...], NT, preferred_element_type=F32
    )
    term_send[...] = terms.astype(BF16).reshape(term_send.shape)

    def term_copy(k):
        return pltpu.make_async_remote_copy(
            src_ref=term_send.at[at_lane(k)], dst_ref=term_recv.at[lane],
            send_sem=term_ss.at[k], recv_sem=term_rs.at[lanes - k],
            device_id={"exp": at_lane(k)}, device_id_type=MESH,
        )

    for k in range(1, lanes):
        term_copy(k).start()
    term_recv[lane] = term_send[lane]

    for k in range(1, lanes):
        peer = at_lane(k)
        pltpu.make_async_remote_copy(
            src_ref=gate_send.at[peer], dst_ref=gate_recv.at[peer],
            send_sem=gate_ss.at[peer], recv_sem=gate_rs.at[peer],
            device_id={"exp": peer}, device_id_type=MESH,
        ).wait_recv()
    gate_rows[...] = jnp.zeros_like(gate_rows)
    for e in range(window):
        gate_rows[e:e + 1, :] = gate_recv[2 * e, 0:1, :] + gate_recv[2 * e + 1, 0:1, :]
    gate_head = gate_ref[:, :128] + jnp.transpose(gate_rows[...])
    gate_grad = jnp.concatenate([gate_head, gate_ref[:, 128:]], axis=1)
    prob = probs[...]
    centre = jnp.sum(prob * gate_grad, axis=1, keepdims=True)
    logit_low = (prob * (gate_grad - centre)).astype(BF16)
    logits_all[0] = logit_low

    def logit_copy(k):
        return pltpu.make_async_remote_copy(
            src_ref=logits_all.at[0], dst_ref=logits_all.at[toks - k],
            send_sem=log_ss.at[k], recv_sem=log_rs.at[toks - k],
            device_id={"tok": at_tok(k)}, device_id_type=MESH,
        )

    for k in range(1, toks):
        logit_copy(k).start()
    xgrad_out[...] = lax.dot_general(logit_low, rw[...], NT, preferred_element_type=F32).astype(BF16)
    for k in range(1, toks):
        logit_copy(k).wait_recv()

    experts = rw.shape[1]
    part = jnp.dot(
        xturned[...], logits_all[...].reshape(toks * rows, experts), preferred_element_type=F32
    ).reshape(outers, 2, own_rows, experts)
    part_mine[...] = jnp.where(inner == 0, part[:, 0], part[:, 1])
    part_send[...] = jnp.where(inner == 0, part[:, 1], part[:, 0]).astype(BF16)
    across = pltpu.make_async_remote_copy(
        src_ref=part_send, dst_ref=part_recv, send_sem=px_ss, recv_sem=px_rs,
        device_id={"exp": outer * 2 + 1 - inner}, device_id_type=MESH,
    )
    across.start()

    for k in range(1, lanes):
        peer = at_lane(k)
        pltpu.make_async_remote_copy(
            src_ref=term_send.at[peer], dst_ref=term_recv.at[peer],
            send_sem=term_ss.at[k], recv_sem=term_rs.at[k],
            device_id={"exp": peer}, device_id_type=MESH,
        ).wait_recv()
    own_hits = own_hits_ref[...]
    own_rank = jnp.dot(own_hits.astype(BF16), before, preferred_element_type=F32) - 1.0
    spread = []
    for e in range(window):
        block = ((own_hits[e:e + 1] > 0.0) & (own_rank[e:e + 1] == slot_iota)).astype(F32)
        spread += [block, block]
    spread = jnp.transpose(jnp.concatenate(spread, axis=0)).astype(BF16)
    latent_out[...] = jnp.dot(
        spread, term_recv[...].reshape(lanes * SLOTS, term_recv.shape[2]), preferred_element_type=F32
    ).astype(BF16)

    across.wait_recv()
    column = part_mine[...] + part_recv[...].astype(F32)
    part_mine[...] = column
    zpart_send[...] = column.astype(BF16)

    def zpart_copy(k):
        peer = lax.rem(outer + k, outers)
        return pltpu.make_async_remote_copy(
            src_ref=zpart_send.at[peer], dst_ref=zpart_recv.at[outers - k],
            send_sem=pz_ss.at[k], recv_sem=pz_rs.at[outers - k],
            device_id={"exp": peer * 2 + inner}, device_id_type=MESH,
        )

    for k in range(1, outers):
        zpart_copy(k).start()
    total = part_mine[outer]
    for k in range(1, outers):
        zpart_copy(k).wait_recv()
    for k in range(1, outers):
        total = total + zpart_recv[k].astype(F32)
    rwg_out[...] = total

    def sent(src_outer, carry):
        for which in range(2):
            forward(which, src_outer, lambda c: c.wait_send())
        return carry

    lax.fori_loop(0, outers, sent, 0)
    for k in range(1, lanes):
        pick_copy(k).wait_send()
        gate_copy(at_lane(k)).wait_send()
        term_copy(k).wait_send()
    for k in range(1, toks):
        band_copy(k).wait_send()
        logit_copy(k).wait_send()
    for k in range(1, outers):
        zpart_copy(k).wait_send()
    across.wait_send()


def shards(
    x_tokens, router_weight, gate_rest, latent_in, latent_grad, expert_picks, expert_in, expert_out
):
    toks = lax.axis_size("tok")
    lanes = lax.axis_size("exp")
    lane = lax.axis_index("exp")
    rows, width = x_tokens.shape
    experts = router_weight.shape[1]
    window = experts - gate_rest.shape[1]
    latent, hidden = expert_in.shape[1:]
    feats = width // toks
    own_rows = feats // lanes
    outers = lanes // 2
    pad = -(-window // 8) * 8
    gate_pad = jnp.pad(gate_rest, ((0, 0), (window, 0)))
    hits = jnp.any(expert_picks == lane // 2, axis=1).astype(F32).reshape(lanes, rows)
    own_picks = lax.dynamic_slice_in_dim(expert_picks, lane * rows, rows, 0)
    ids = jnp.where(jnp.arange(pad) < window, jnp.arange(pad), -1)
    own_hits = jnp.any(own_picks[None] == ids[:, None, None], axis=2).astype(F32)
    vmem = pl.BlockSpec(memory_space=pltpu.VMEM)
    anywhere = pl.BlockSpec(memory_space=pl.ANY)
    dma = pltpu.SemaphoreType.DMA
    return pl.pallas_call(
        functools.partial(kernel, toks, lanes, window),
        out_shape=(
            jax.ShapeDtypeStruct((rows, latent), BF16),
            jax.ShapeDtypeStruct((rows, width), BF16),
            jax.ShapeDtypeStruct((own_rows, experts), F32),
        ),
        in_specs=[vmem] * 6 + [anywhere] * 3,
        out_specs=(vmem, vmem, vmem),
        scratch_shapes=[
            pltpu.VMEM((width, experts), BF16),
            pltpu.VMEM((latent, hidden), BF16),
            pltpu.VMEM((hidden, latent), BF16),
            pltpu.VMEM((2, lanes, rows, latent), BF16),
            pltpu.VMEM((rows, experts), F32),
            pltpu.VMEM((lanes, pad, rows), F32),
            pltpu.VMEM((pad, rows), F32),
            pltpu.VMEM((lanes, 8, rows), F32),
            pltpu.VMEM((lanes, 8, rows), F32),
            pltpu.VMEM((128, rows), F32),
            pltpu.VMEM((lanes, rows), F32),
            pltpu.VMEM((lanes, SLOTS, hidden), BF16),
            pltpu.VMEM((lanes, SLOTS, latent), BF16),
            pltpu.VMEM((lanes, SLOTS, latent), BF16),
            pltpu.VMEM((toks, rows, feats), BF16),
            pltpu.VMEM((feats, toks * rows), BF16),
            pltpu.VMEM((toks, rows, experts), BF16),
            pltpu.VMEM((outers, own_rows, experts), F32),
            pltpu.VMEM((outers, own_rows, experts), BF16),
            pltpu.VMEM((outers, own_rows, experts), BF16),
            pltpu.VMEM((outers, own_rows, experts), BF16),
            pltpu.VMEM((outers, own_rows, experts), BF16),
            dma((3,)),
            dma((3, 2, outers)),
            dma((2, outers)),
            dma((2, outers)),
            dma((lanes,)), dma((lanes,)),
            dma((lanes,)), dma((lanes,)),
            dma((lanes,)), dma((lanes,)),
            dma((toks,)), dma((toks,)),
            dma((toks,)), dma((toks,)),
            dma, dma,
            dma((outers,)), dma((outers,)),
        ],
        compiler_params=pltpu.CompilerParams(
            collective_id=0, has_side_effects=True, vmem_limit_bytes=56 * 1024 * 1024
        ),
    )(x_tokens, gate_pad, latent_in, latent_grad, hits, own_hits, router_weight, expert_in, expert_out)


def solution(mesh):
    placed = (
        P(("tok", "exp"), None),
        P(),
        P(("tok", "exp"), None),
        P(("tok", "exp"), None),
        P(("tok", "exp"), None),
        P("tok", None),
        P("exp", None, None),
        P("exp", None, None),
    )
    return jax.shard_map(
        shards,
        mesh=mesh,
        in_specs=placed,
        out_specs=(P(("tok", "exp"), None), P(("tok", "exp"), None), P(("tok", "exp"), None)),
        check_vma=False,
    )
```

```python
import functools
import jax
import jax.numpy as jnp
from jax import lax
from jax.experimental import pallas as pl
from jax.experimental.pallas import tpu as pltpu
from jax.sharding import PartitionSpec as P

MESH = pl.DeviceIdType.MESH
F32 = jnp.float32
BF16 = jnp.bfloat16
NT = (((1,), (1,)), ((), ()))
SLOTS = 16


def kernel(
    toks, lanes, window,
    x_ref, gate_ref, latin_ref, latgrad_ref, picks_ref, rw_hbm, win_hbm, wout_hbm,
    latent_out, xgrad_out, rwg_out,
    rw, win, wout, lat, probs, pick_recv, pick_send, gate_recv, gate_send, gate_rows, gate_grads, hits_ref, own_hits_ref, rank, packed,
    term_send, term_recv, xband, xturned, logits_all, part_mine, part_send, part_recv,
    zpart_send, zpart_recv,
    load_sem, send_lat, chain_ss, recv_z, recv_x, pick_ss, pick_rs, gate_ss, gate_rs, term_ss, term_rs,
    band_ss, band_rs, log_ss, log_rs, px_ss, px_rs, pz_ss, pz_rs,
):
    tok = lax.axis_index("tok")
    lane = lax.axis_index("exp")
    outers = lanes // 2
    outer = lane // 2
    inner = lane % 2
    expert = lane // 2
    rows = x_ref.shape[0]
    feats = x_ref.shape[1] // toks
    own_rows = feats // lanes

    loads = [
        pltpu.make_async_copy(rw_hbm, rw, load_sem.at[0]),
        pltpu.make_async_copy(win_hbm.at[0], win, load_sem.at[1]),
        pltpu.make_async_copy(wout_hbm.at[0], wout, load_sem.at[2]),
    ]
    for load in loads:
        load.start()

    def at_lane(k):
        return lax.rem(lane + k, lanes)

    def at_tok(k):
        return lax.rem(tok + k, toks)

    barrier = pltpu.get_barrier_semaphore()
    for k in range(1, lanes):
        pl.semaphore_signal(barrier, inc=1, device_id={"exp": at_lane(k)}, device_id_type=MESH)
    for k in range(1, toks):
        pl.semaphore_signal(barrier, inc=1, device_id={"tok": at_tok(k)}, device_id_type=MESH)
    lat[0, lane] = latin_ref[...]
    lat[1, lane] = latgrad_ref[...]
    pl.semaphore_wait(barrier, lanes - 1 + toks - 1)

    def lat_copy(kind, which, src_outer, src_inner):
        slot = src_outer * 2 + src_inner
        if kind == 2:
            peer, recv = outer * 2 + 1 - inner, recv_x.at[which, src_outer]
        else:
            peer, recv = lane + (2 if kind == 0 else -2), recv_z.at[which, src_outer]
        return pltpu.make_async_remote_copy(
            src_ref=lat.at[which, slot], dst_ref=lat.at[which, slot],
            send_sem=send_lat.at[kind, which, src_outer], recv_sem=recv,
            device_id={"exp": peer}, device_id_type=MESH,
        )

    def forward(which, src_outer, do):
        @pl.when((src_outer <= outer) & (outer < outers - 1))
        def _():
            do(lat_copy(0, which, src_outer, inner))

        @pl.when((src_outer >= outer) & (outer > 0))
        def _():
            do(lat_copy(1, which, src_outer, inner))

        if which == 0:
            do(lat_copy(2, which, src_outer, inner))
        else:
            @pl.when((src_outer == outer) | ((src_outer > 0) & (src_outer < outers - 1)))
            def _():
                do(lat_copy(2, which, src_outer, inner))

    def chain(src_outer, do):
        slot = src_outer * 2 + 1 - inner
        for side, end in ((1, 0), (-1, outers - 1)):
            @pl.when((src_outer == end) & (outer + side >= 0) & (outer + side < outers))
            def _():
                do(pltpu.make_async_remote_copy(
                    src_ref=lat.at[1, slot], dst_ref=lat.at[1, slot],
                    send_sem=chain_ss.at[0 if side == 1 else 1], recv_sem=recv_x.at[1, src_outer],
                    device_id={"exp": lane + 2 * side}, device_id_type=MESH,
                ))

    for which in range(2):
        forward(which, outer, lambda c: c.start())

    def band_copy(k):
        peer = at_tok(k)
        return pltpu.make_async_remote_copy(
            src_ref=x_ref.at[:, pl.ds(pl.multiple_of(peer * feats, 128), feats)],
            dst_ref=xband.at[tok],
            send_sem=band_ss.at[k], recv_sem=band_rs.at[toks - k],
            device_id={"tok": peer}, device_id_type=MESH,
        )

    for k in range(1, toks):
        band_copy(k).start()
    xband[tok] = x_ref[:, pl.ds(pl.multiple_of(tok * feats, 128), feats)]

    def any_row(picks, e):
        return jnp.max((picks == e).astype(F32), axis=0, keepdims=True)

    group_hits = any_row(picks_ref[...], expert)
    for k in range(lanes):
        hits_ref[k:k + 1, :] = group_hits[:, k * rows:(k + 1) * rows]
    own_picks = picks_ref[:, pl.ds(pl.multiple_of(lane * rows, rows), rows)]
    own_hits_ref[...] = jnp.zeros_like(own_hits_ref)
    for e in range(window):
        own_hits_ref[e:e + 1, :] = any_row(own_picks, e)
    rest = gate_ref.shape[1]
    gate_grads[:, rest - rest % 128:] = jnp.zeros_like(gate_grads[:, rest - rest % 128:])
    gate_grads[:, :rest] = gate_ref[...]
    gate_grads[...] = pltpu.roll(gate_grads[...], window, 1)

    loads[0].wait()
    logits = jnp.dot(x_ref[...], rw[...], preferred_element_type=F32)
    shifted = jnp.exp(logits - jnp.max(logits, axis=1, keepdims=True))
    probs[...] = shifted / jnp.sum(shifted, axis=1, keepdims=True)
    pad = own_hits_ref.shape[0]
    pick_send[...] = jnp.transpose(probs[:, :128])[:pad] * own_hits_ref[...]
    pick_recv[0] = pick_send[...]

    def pick_copy(k):
        return pltpu.make_async_remote_copy(
            src_ref=pick_send, dst_ref=pick_recv.at[lanes - k],
            send_sem=pick_ss.at[k], recv_sem=pick_rs.at[lanes - k],
            device_id={"exp": at_lane(k)}, device_id_type=MESH,
        )

    for k in range(1, lanes):
        pick_copy(k).start()
    before = (
        lax.broadcasted_iota(jnp.int32, (rows, rows), 0)
        <= lax.broadcasted_iota(jnp.int32, (rows, rows), 1)
    ).astype(BF16)
    rank[...] = jnp.dot(hits_ref[...].astype(BF16), before, preferred_element_type=F32) - 1.0
    slot_iota = lax.broadcasted_iota(jnp.int32, (SLOTS, rows), 0).astype(F32)
    loads[1].wait()
    loads[2].wait()
    for k in range(1, lanes):
        pick_copy(k).wait_recv()

    def gate_copy(src_lane):
        return pltpu.make_async_remote_copy(
            src_ref=gate_send.at[src_lane], dst_ref=gate_recv.at[lane],
            send_sem=gate_ss.at[src_lane], recv_sem=gate_rs.at[lane],
            device_id={"exp": src_lane}, device_id_type=MESH,
        )

    def expert_rows(src_lane):
        active = jnp.maximum(lax.dot_general(lat[0, src_lane], win[...], NT, preferred_element_type=F32), 0.0)
        grad = lax.dot_general(lat[1, src_lane], wout[...], NT, preferred_element_type=F32)
        product = active * grad
        gate = jnp.sum(active * product, axis=1, keepdims=True)
        gate_row = jnp.transpose(jnp.broadcast_to(gate, (rows, rows)))[:8]
        gate_send[src_lane] = gate_row

        @pl.when(src_lane == lane)
        def _():
            gate_recv[lane] = gate_row

        @pl.when(src_lane != lane)
        def _():
            gate_copy(src_lane).start()

        chosen = (
            (hits_ref[pl.ds(src_lane, 1), :] > 0.0) & (rank[pl.ds(src_lane, 1), :] == slot_iota)
        ).astype(F32)
        picked = pick_recv[lax.rem(src_lane - lane + lanes, lanes), pl.ds(expert, 1), :]
        scale = jnp.sum(chosen * picked, axis=1, keepdims=True)
        raw = jnp.dot(chosen.astype(BF16), (2.0 * product).astype(BF16), preferred_element_type=F32)
        packed[src_lane] = (raw * scale).astype(BF16)

    def arrivals(step, carry):
        for side in (-1, 1):
            src_outer = outer + side * step

            @pl.when((step > 0) & (step < outers) & (src_outer >= 0) & (src_outer < outers))
            def _():
                for which in range(2):
                    lat_copy(0, which, src_outer, inner).wait_recv()
                    forward(which, src_outer, lambda c: c.start())

        def piece(q, carry):
            across = q // 2
            side = q % 2
            distance = step - across
            src_outer = outer + (2 * side - 1) * distance
            valid = (src_outer >= 0) & (src_outer < outers) & (distance >= 0)
            valid = valid & ((distance > 0) | (side == 0)) & (distance < outers)

            @pl.when(valid & (across == 1))
            def _():
                for which in range(2):
                    lat_copy(2, which, src_outer, 1 - inner).wait_recv()
                chain(src_outer, lambda c: c.start())

            @pl.when(valid)
            def _():
                expert_rows(src_outer * 2 + lax.rem(inner + across, 2))

            return carry

        lax.fori_loop(0, 4, piece, 0)

        @pl.when(step == outers - 1)
        def _():
            for k in range(toks):
                if k:
                    band_copy(k).wait_recv()
            for k in range(toks):
                xturned[:, k * rows:(k + 1) * rows] = jnp.transpose(xband[k])

        return carry

    lax.fori_loop(0, outers + 1, arrivals, 0)

    terms = jnp.dot(
        packed[...].reshape(lanes * SLOTS, packed.shape[2]), win[...], preferred_element_type=F32
    )
    term_send[...] = terms.astype(BF16).reshape(term_send.shape)

    def term_copy(k):
        return pltpu.make_async_remote_copy(
            src_ref=term_send.at[at_lane(k)], dst_ref=term_recv.at[lane],
            send_sem=term_ss.at[k], recv_sem=term_rs.at[lanes - k],
            device_id={"exp": at_lane(k)}, device_id_type=MESH,
        )

    for k in range(1, lanes):
        term_copy(k).start()
    term_recv[lane] = term_send[lane]

    for k in range(1, lanes):
        peer = at_lane(k)
        pltpu.make_async_remote_copy(
            src_ref=gate_send.at[peer], dst_ref=gate_recv.at[peer],
            send_sem=gate_ss.at[peer], recv_sem=gate_rs.at[peer],
            device_id={"exp": peer}, device_id_type=MESH,
        ).wait_recv()
    gate_rows[...] = jnp.zeros_like(gate_rows)
    for e in range(window):
        gate_rows[e:e + 1, :] = gate_recv[2 * e, 0:1, :] + gate_recv[2 * e + 1, 0:1, :]
    gate_grads[:, :128] = gate_grads[:, :128] + jnp.transpose(gate_rows[...])
    gate_grad = gate_grads[...]
    prob = probs[...]
    centre = jnp.sum(prob * gate_grad, axis=1, keepdims=True)
    logit_low = (prob * (gate_grad - centre)).astype(BF16)
    logits_all[tok] = logit_low
    sibling = tok + 1 - 2 * lax.rem(tok, 2)

    def logit_copy(to_sibling, k):
        far = lax.rem(tok + 2 * k, toks)
        src = far if to_sibling else tok
        sem = (toks // 2 + k) if to_sibling else (toks // 2 - k) % (toks // 2)
        return pltpu.make_async_remote_copy(
            src_ref=logits_all.at[src], dst_ref=logits_all.at[src],
            send_sem=log_ss.at[toks // 2 + k if to_sibling else k], recv_sem=log_rs.at[sem],
            device_id={"tok": sibling if to_sibling else far}, device_id_type=MESH,
        )

    for k in range(1, toks // 2):
        logit_copy(False, k).start()
    logit_copy(True, 0).start()
    xgrad_out[...] = lax.dot_general(logit_low, rw[...], NT, preferred_element_type=F32).astype(BF16)
    for k in range(toks // 2 - 1, 0, -1):
        logit_copy(False, toks // 2 - k).wait_recv()
        logit_copy(True, k).start()
    for k in range(toks // 2):
        logit_copy(True, k).wait_recv()

    experts = rw.shape[1]
    part = jnp.dot(
        xturned[...], logits_all[...].reshape(toks * rows, experts), preferred_element_type=F32
    ).reshape(outers, 2, own_rows, experts)
    part_mine[...] = jnp.where(inner == 0, part[:, 0], part[:, 1])
    part_send[...] = jnp.where(inner == 0, part[:, 1], part[:, 0]).astype(BF16)
    across = pltpu.make_async_remote_copy(
        src_ref=part_send, dst_ref=part_recv, send_sem=px_ss, recv_sem=px_rs,
        device_id={"exp": outer * 2 + 1 - inner}, device_id_type=MESH,
    )
    across.start()

    for k in range(1, lanes):
        peer = at_lane(k)
        pltpu.make_async_remote_copy(
            src_ref=term_send.at[peer], dst_ref=term_recv.at[peer],
            send_sem=term_ss.at[k], recv_sem=term_rs.at[k],
            device_id={"exp": peer}, device_id_type=MESH,
        ).wait_recv()
    own_hits = own_hits_ref[...]
    own_rank = jnp.dot(own_hits.astype(BF16), before, preferred_element_type=F32) - 1.0
    spread = []
    for e in range(window):
        block = ((own_hits[e:e + 1] > 0.0) & (own_rank[e:e + 1] == slot_iota)).astype(F32)
        spread += [block, block]
    spread = jnp.transpose(jnp.concatenate(spread, axis=0)).astype(BF16)
    latent_out[...] = jnp.dot(
        spread, term_recv[...].reshape(lanes * SLOTS, term_recv.shape[2]), preferred_element_type=F32
    ).astype(BF16)

    across.wait_recv()
    column = part_mine[...] + part_recv[...].astype(F32)
    part_mine[...] = column
    zpart_send[...] = column.astype(BF16)

    def zpart_copy(k):
        peer = lax.rem(outer + k, outers)
        return pltpu.make_async_remote_copy(
            src_ref=zpart_send.at[peer], dst_ref=zpart_recv.at[outers - k],
            send_sem=pz_ss.at[k], recv_sem=pz_rs.at[outers - k],
            device_id={"exp": peer * 2 + inner}, device_id_type=MESH,
        )

    for k in range(1, outers):
        zpart_copy(k).start()
    total = part_mine[outer]
    for k in range(1, outers):
        zpart_copy(k).wait_recv()
    for k in range(1, outers):
        total = total + zpart_recv[k].astype(F32)
    rwg_out[...] = total

    def sent(src_outer, carry):
        for which in range(2):
            forward(which, src_outer, lambda c: c.wait_send())
        chain(src_outer, lambda c: c.wait_send())
        return carry

    lax.fori_loop(0, outers, sent, 0)
    for k in range(1, lanes):
        pick_copy(k).wait_send()
        gate_copy(at_lane(k)).wait_send()
        term_copy(k).wait_send()
    for k in range(1, toks):
        band_copy(k).wait_send()
    for k in range(1, outers):
        zpart_copy(k).wait_send()
    across.wait_send()
    for k in range(toks // 2):
        logit_copy(True, k).wait_send()
        if k:
            logit_copy(False, k).wait_send()


def shards(
    x_tokens, router_weight, gate_rest, latent_in, latent_grad, expert_picks, expert_in, expert_out
):
    toks = lax.axis_size("tok")
    lanes = lax.axis_size("exp")
    rows, width = x_tokens.shape
    experts = router_weight.shape[1]
    window = experts - gate_rest.shape[1]
    latent, hidden = expert_in.shape[1:]
    feats = width // toks
    own_rows = feats // lanes
    outers = lanes // 2
    pad = -(-window // 8) * 8
    vmem = pl.BlockSpec(memory_space=pltpu.VMEM)
    anywhere = pl.BlockSpec(memory_space=pl.ANY)
    dma = pltpu.SemaphoreType.DMA
    return pl.pallas_call(
        functools.partial(kernel, toks, lanes, window),
        out_shape=(
            jax.ShapeDtypeStruct((rows, latent), BF16),
            jax.ShapeDtypeStruct((rows, width), BF16),
            jax.ShapeDtypeStruct((own_rows, experts), F32),
        ),
        in_specs=[vmem] * 5 + [anywhere] * 3,
        out_specs=(vmem, vmem, vmem),
        scratch_shapes=[
            pltpu.VMEM((width, experts), BF16),
            pltpu.VMEM((hidden, latent), BF16),
            pltpu.VMEM((hidden, latent), BF16),
            pltpu.VMEM((2, lanes, rows, latent), BF16),
            pltpu.VMEM((rows, experts), F32),
            pltpu.VMEM((lanes, pad, rows), F32),
            pltpu.VMEM((pad, rows), F32),
            pltpu.VMEM((lanes, 8, rows), F32),
            pltpu.VMEM((lanes, 8, rows), F32),
            pltpu.VMEM((128, rows), F32),
            pltpu.VMEM((rows, experts), F32),
            pltpu.VMEM((lanes, rows), F32),
            pltpu.VMEM((pad, rows), F32),
            pltpu.VMEM((lanes, rows), F32),
            pltpu.VMEM((lanes, SLOTS, hidden), BF16),
            pltpu.VMEM((lanes, SLOTS, latent), BF16),
            pltpu.VMEM((lanes, SLOTS, latent), BF16),
            pltpu.VMEM((toks, rows, feats), BF16),
            pltpu.VMEM((feats, toks * rows), BF16),
            pltpu.VMEM((toks, rows, experts), BF16),
            pltpu.VMEM((outers, own_rows, experts), F32),
            pltpu.VMEM((outers, own_rows, experts), BF16),
            pltpu.VMEM((outers, own_rows, experts), BF16),
            pltpu.VMEM((outers, own_rows, experts), BF16),
            pltpu.VMEM((outers, own_rows, experts), BF16),
            dma((3,)),
            dma((3, 2, outers)),
            dma((2,)),
            dma((2, outers)),
            dma((2, outers)),
            dma((lanes,)), dma((lanes,)),
            dma((lanes,)), dma((lanes,)),
            dma((lanes,)), dma((lanes,)),
            dma((toks,)), dma((toks,)),
            dma((toks,)), dma((toks,)),
            dma, dma,
            dma((outers,)), dma((outers,)),
        ],
        compiler_params=pltpu.CompilerParams(
            collective_id=0, has_side_effects=True, vmem_limit_bytes=56 * 1024 * 1024
        ),
    )(
        x_tokens, gate_rest, latent_in, latent_grad, expert_picks.T, router_weight,
        jnp.swapaxes(expert_in, 1, 2), expert_out,
    )


def solution(mesh):
    placed = (
        P(("tok", "exp"), None),
        P(),
        P(("tok", "exp"), None),
        P(("tok", "exp"), None),
        P(("tok", "exp"), None),
        P("tok", None),
        P("exp", None, None),
        P("exp", None, None),
    )
    return jax.shard_map(
        shards,
        mesh=mesh,
        in_specs=placed,
        out_specs=(P(("tok", "exp"), None), P(("tok", "exp"), None), P(("tok", "exp"), None)),
        check_vma=False,
    )
```

```python
import functools
import jax
import jax.numpy as jnp
from jax import lax
from jax.experimental import pallas as pl
from jax.experimental.pallas import tpu as pltpu
from jax.sharding import PartitionSpec as P

MESH = pl.DeviceIdType.MESH
F32 = jnp.float32
BF16 = jnp.bfloat16
NT = (((1,), (1,)), ((), ()))
SLOTS = 16


def kernel(
    toks, lanes, window,
    x_ref, gate_ref, latin_ref, latgrad_ref, picks_ref, rw_hbm, win_hbm, wout_hbm,
    latent_out, xgrad_out, rwg_out,
    rw, win, wout, lat, probs, pick_recv, pick_send, gate_recv, gate_send, gate_rows, gate_grads, hits_ref, own_hits_ref, rank, packed,
    term_send, term_recv, xband, xturned, logits_all, part, ax_send, ax_recv,
    bz_send, bz_recv, bx_send, bx_recv, az_send, az_recv, total_a, total_b,
    load_sem, send_lat, chain_ss, recv_z, recv_x, pick_ss, pick_rs, gate_ss, gate_rs, term_ss, term_rs,
    band_ss, band_rs, log_ss, log_rs, ax_ss, ax_rs, bz_ss, bz_rs, bx_ss, bx_rs,
    az_ss, az_rs,
):
    tok = lax.axis_index("tok")
    lane = lax.axis_index("exp")
    outers = lanes // 2
    outer = lane // 2
    inner = lane % 2
    expert = lane // 2
    rows = x_ref.shape[0]
    feats = x_ref.shape[1] // toks
    half = feats // lanes // 2

    loads = [
        pltpu.make_async_copy(rw_hbm, rw, load_sem.at[0]),
        pltpu.make_async_copy(win_hbm.at[0], win, load_sem.at[1]),
        pltpu.make_async_copy(wout_hbm.at[0], wout, load_sem.at[2]),
    ]
    for load in loads:
        load.start()

    def at_lane(k):
        return lax.rem(lane + k, lanes)

    def at_tok(k):
        return lax.rem(tok + k, toks)

    barrier = pltpu.get_barrier_semaphore()
    for k in range(1, lanes):
        pl.semaphore_signal(barrier, inc=1, device_id={"exp": at_lane(k)}, device_id_type=MESH)
    for k in range(1, toks):
        pl.semaphore_signal(barrier, inc=1, device_id={"tok": at_tok(k)}, device_id_type=MESH)
    lat[0, lane] = latin_ref[...]
    lat[1, lane] = latgrad_ref[...]
    pl.semaphore_wait(barrier, lanes - 1 + toks - 1)

    def lat_copy(kind, which, src_outer, src_inner):
        slot = src_outer * 2 + src_inner
        if kind == 2:
            peer, recv = outer * 2 + 1 - inner, recv_x.at[which, src_outer]
        else:
            peer, recv = lane + (2 if kind == 0 else -2), recv_z.at[which, src_outer]
        return pltpu.make_async_remote_copy(
            src_ref=lat.at[which, slot], dst_ref=lat.at[which, slot],
            send_sem=send_lat.at[kind, which, src_outer], recv_sem=recv,
            device_id={"exp": peer}, device_id_type=MESH,
        )

    def forward(which, src_outer, do):
        @pl.when((src_outer <= outer) & (outer < outers - 1))
        def _():
            do(lat_copy(0, which, src_outer, inner))

        @pl.when((src_outer >= outer) & (outer > 0))
        def _():
            do(lat_copy(1, which, src_outer, inner))

        if which == 0:
            do(lat_copy(2, which, src_outer, inner))
        else:
            @pl.when((src_outer == outer) | ((src_outer > 0) & (src_outer < outers - 1)))
            def _():
                do(lat_copy(2, which, src_outer, inner))

    def chain(src_outer, do):
        slot = src_outer * 2 + 1 - inner
        for side, end in ((1, 0), (-1, outers - 1)):
            @pl.when((src_outer == end) & (outer + side >= 0) & (outer + side < outers))
            def _():
                do(pltpu.make_async_remote_copy(
                    src_ref=lat.at[1, slot], dst_ref=lat.at[1, slot],
                    send_sem=chain_ss.at[0 if side == 1 else 1], recv_sem=recv_x.at[1, src_outer],
                    device_id={"exp": lane + 2 * side}, device_id_type=MESH,
                ))

    for which in range(2):
        forward(which, outer, lambda c: c.start())

    def band_copy(k):
        peer = at_tok(k)
        return pltpu.make_async_remote_copy(
            src_ref=x_ref.at[:, pl.ds(pl.multiple_of(peer * feats, 128), feats)],
            dst_ref=xband.at[tok],
            send_sem=band_ss.at[k], recv_sem=band_rs.at[toks - k],
            device_id={"tok": peer}, device_id_type=MESH,
        )

    for k in range(1, toks):
        band_copy(k).start()
    xband[tok] = x_ref[:, pl.ds(pl.multiple_of(tok * feats, 128), feats)]

    def any_row(picks, e):
        return jnp.max((picks == e).astype(F32), axis=0, keepdims=True)

    group_hits = any_row(picks_ref[...], expert)
    for k in range(lanes):
        hits_ref[k:k + 1, :] = group_hits[:, k * rows:(k + 1) * rows]
    own_picks = picks_ref[:, pl.ds(pl.multiple_of(lane * rows, rows), rows)]
    own_hits_ref[...] = jnp.zeros_like(own_hits_ref)
    for e in range(window):
        own_hits_ref[e:e + 1, :] = any_row(own_picks, e)
    rest = gate_ref.shape[1]
    gate_grads[:, rest - rest % 128:] = jnp.zeros_like(gate_grads[:, rest - rest % 128:])
    gate_grads[:, :rest] = gate_ref[...]
    gate_grads[...] = pltpu.roll(gate_grads[...], window, 1)

    loads[0].wait()
    logits = jnp.dot(x_ref[...], rw[...], preferred_element_type=F32)
    shifted = jnp.exp(logits - jnp.max(logits, axis=1, keepdims=True))
    probs[...] = shifted / jnp.sum(shifted, axis=1, keepdims=True)
    pad = own_hits_ref.shape[0]
    pick_send[...] = jnp.transpose(probs[:, :128])[:pad] * own_hits_ref[...]
    pick_recv[0] = pick_send[...]

    def pick_copy(k):
        return pltpu.make_async_remote_copy(
            src_ref=pick_send, dst_ref=pick_recv.at[lanes - k],
            send_sem=pick_ss.at[k], recv_sem=pick_rs.at[lanes - k],
            device_id={"exp": at_lane(k)}, device_id_type=MESH,
        )

    for k in range(1, lanes):
        pick_copy(k).start()
    before = (
        lax.broadcasted_iota(jnp.int32, (rows, rows), 0)
        <= lax.broadcasted_iota(jnp.int32, (rows, rows), 1)
    ).astype(BF16)
    rank[...] = jnp.dot(hits_ref[...].astype(BF16), before, preferred_element_type=F32) - 1.0
    slot_iota = lax.broadcasted_iota(jnp.int32, (SLOTS, rows), 0).astype(F32)
    loads[1].wait()
    loads[2].wait()
    for k in range(1, lanes):
        pick_copy(k).wait_recv()

    def gate_copy(src_lane):
        return pltpu.make_async_remote_copy(
            src_ref=gate_send.at[src_lane], dst_ref=gate_recv.at[lane],
            send_sem=gate_ss.at[src_lane], recv_sem=gate_rs.at[lane],
            device_id={"exp": src_lane}, device_id_type=MESH,
        )

    def pair_rows(src_outer):
        first = src_outer * 2
        both = lat.shape[3]
        rows_in = lat[0, pl.ds(first, 2)].reshape(2 * rows, both)
        rows_grad = lat[1, pl.ds(first, 2)].reshape(2 * rows, both)
        active = jnp.maximum(lax.dot_general(rows_in, win[...], NT, preferred_element_type=F32), 0.0)
        grad = lax.dot_general(rows_grad, wout[...], NT, preferred_element_type=F32)
        product = active * grad
        gate = jnp.sum(active * product, axis=1, keepdims=True)
        gate_row = jnp.transpose(jnp.broadcast_to(gate, (2 * rows, 128)))[:8]
        for side in range(2):
            gate_send[first + side] = gate_row[:, side * rows:(side + 1) * rows]

            @pl.when(first + side == lane)
            def _():
                gate_recv[lane] = gate_row[:, side * rows:(side + 1) * rows]

            @pl.when(first + side != lane)
            def _():
                gate_copy(first + side).start()

        raw_rows = (2.0 * product).astype(BF16)
        for side in range(2):
            src_lane = first + side
            chosen = (
                (hits_ref[pl.ds(src_lane, 1), :] > 0.0) & (rank[pl.ds(src_lane, 1), :] == slot_iota)
            ).astype(F32)
            picked = pick_recv[lax.rem(src_lane - lane + lanes, lanes), pl.ds(expert, 1), :]
            scale = jnp.sum(chosen * picked, axis=1, keepdims=True)
            raw = jnp.dot(
                chosen.astype(BF16), raw_rows[side * rows:(side + 1) * rows], preferred_element_type=F32
            )
            packed[src_lane] = (raw * scale).astype(BF16)

    def arrivals(step, carry):
        for side in (-1, 1):
            src_outer = outer + side * step

            @pl.when((step > 0) & (step < outers) & (src_outer >= 0) & (src_outer < outers))
            def _():
                for which in range(2):
                    lat_copy(0, which, src_outer, inner).wait_recv()
                    forward(which, src_outer, lambda c: c.start())

        def pair(q, carry):
            distance = step - 1
            src_outer = outer + (2 * q - 1) * distance
            valid = (src_outer >= 0) & (src_outer < outers) & (distance >= 0)
            valid = valid & ((distance > 0) | (q == 0))

            @pl.when(valid)
            def _():
                for which in range(2):
                    lat_copy(2, which, src_outer, 1 - inner).wait_recv()
                chain(src_outer, lambda c: c.start())
                pair_rows(src_outer)

            return carry

        lax.fori_loop(0, 2, pair, 0)

        @pl.when(step == outers - 1)
        def _():
            for k in range(toks):
                if k:
                    band_copy(k).wait_recv()
            for k in range(toks):
                xturned[:, k * rows:(k + 1) * rows] = jnp.transpose(xband[k])

        return carry

    lax.fori_loop(0, outers + 1, arrivals, 0)

    terms = jnp.dot(
        packed[...].reshape(lanes * SLOTS, packed.shape[2]), win[...], preferred_element_type=F32
    )
    term_send[...] = terms.astype(BF16).reshape(term_send.shape)

    def term_copy(k):
        return pltpu.make_async_remote_copy(
            src_ref=term_send.at[at_lane(k)], dst_ref=term_recv.at[lane],
            send_sem=term_ss.at[k], recv_sem=term_rs.at[lanes - k],
            device_id={"exp": at_lane(k)}, device_id_type=MESH,
        )

    for k in range(1, lanes):
        term_copy(k).start()
    term_recv[lane] = term_send[lane]

    for k in range(1, lanes):
        peer = at_lane(k)
        pltpu.make_async_remote_copy(
            src_ref=gate_send.at[peer], dst_ref=gate_recv.at[peer],
            send_sem=gate_ss.at[peer], recv_sem=gate_rs.at[peer],
            device_id={"exp": peer}, device_id_type=MESH,
        ).wait_recv()
    gate_rows[...] = jnp.zeros_like(gate_rows)
    for e in range(window):
        gate_rows[e:e + 1, :] = gate_recv[2 * e, 0:1, :] + gate_recv[2 * e + 1, 0:1, :]
    gate_grads[:, :128] = gate_grads[:, :128] + jnp.transpose(gate_rows[...])
    gate_grad = gate_grads[...]
    prob = probs[...]
    centre = jnp.sum(prob * gate_grad, axis=1, keepdims=True)
    logit_low = (prob * (gate_grad - centre)).astype(BF16)
    logits_all[tok] = logit_low
    sibling = tok + 1 - 2 * lax.rem(tok, 2)

    def logit_copy(to_sibling, k):
        far = lax.rem(tok + 2 * k, toks)
        src = far if to_sibling else tok
        sem = (toks // 2 + k) if to_sibling else (toks // 2 - k) % (toks // 2)
        return pltpu.make_async_remote_copy(
            src_ref=logits_all.at[src], dst_ref=logits_all.at[src],
            send_sem=log_ss.at[toks // 2 + k if to_sibling else k], recv_sem=log_rs.at[sem],
            device_id={"tok": sibling if to_sibling else far}, device_id_type=MESH,
        )

    for k in range(1, toks // 2):
        logit_copy(False, k).start()
    logit_copy(True, 0).start()
    xgrad_out[...] = lax.dot_general(logit_low, rw[...], NT, preferred_element_type=F32).astype(BF16)
    for k in range(toks // 2 - 1, 0, -1):
        logit_copy(False, toks // 2 - k).wait_recv()
        logit_copy(True, k).start()
    for k in range(toks // 2):
        logit_copy(True, k).wait_recv()

    experts = rw.shape[1]
    part[...] = jnp.dot(
        xturned[...], logits_all[...].reshape(toks * rows, experts), preferred_element_type=F32
    ).reshape(part.shape)
    neighbour = outer * 2 + 1 - inner

    def ax_copy(d):
        return pltpu.make_async_remote_copy(
            src_ref=ax_send.at[d], dst_ref=ax_recv.at[d], send_sem=ax_ss.at[d], recv_sem=ax_rs.at[d],
            device_id={"exp": neighbour}, device_id_type=MESH,
        )

    for d in range(outers):
        ax_send[d] = part[d, 1 - inner, :half].astype(BF16)
        ax_copy(d).start()

    def line_copy(send, recv, ss, rs, way, side, d):
        return pltpu.make_async_remote_copy(
            src_ref=send.at[way, d], dst_ref=recv.at[way, d], send_sem=ss.at[way, d],
            recv_sem=rs.at[way, d], device_id={"exp": lane + 2 * side}, device_id_type=MESH,
        )

    def line_item(m):
        j, q = m // 2, m % 2
        side = (1 - 2 * ((outer * 2) // outers)) * (1 - 2 * q)
        d = ((side + 1) // 2) * (outers - 1 - 2 * j) + j
        return (1 - side) // 2, side, d

    def line(send, recv, ss, rs, own):
        def item(m, carry):
            way, side, d = line_item(m)
            ahead = (d - outer) * side > 0
            behind = (outer - side >= 0) & (outer - side < outers)

            @pl.when(ahead & behind)
            def _():
                line_copy(send, recv, ss, rs, way, side, d).wait_recv()
                send[way, d] = (own(d) + recv[way, d].astype(F32)).astype(BF16)

            @pl.when(ahead & jnp.logical_not(behind))
            def _():
                send[way, d] = own(d).astype(BF16)

            @pl.when(ahead)
            def _():
                line_copy(send, recv, ss, rs, way, side, d).start()

            return carry

        lax.fori_loop(0, 2 * outers, item, 0)

    def line_end(send, recv, ss, rs, total):
        for way, side in ((0, 1), (1, -1)):
            @pl.when((outer - side >= 0) & (outer - side < outers))
            def _():
                line_copy(send, recv, ss, rs, way, side, outer).wait_recv()
                total[...] = total[...] + recv[way, outer].astype(F32)

    def line_sent(send, recv, ss, rs):
        def item(m, carry):
            way, side, d = line_item(m)

            @pl.when((d - outer) * side > 0)
            def _():
                line_copy(send, recv, ss, rs, way, side, d).wait_send()

            return carry

        lax.fori_loop(0, 2 * outers, item, 0)

    line_b = (bz_send, bz_recv, bz_ss, bz_rs)
    line_a = (az_send, az_recv, az_ss, az_rs)
    line(*line_b, lambda d: part[d, :, half:])
    for d in range(outers):
        ax_copy(d).wait_recv()
        part[d, inner, :half] = part[d, inner, :half] + ax_recv[d].astype(F32)
    line(*line_a, lambda d: part[d, inner, :half])
    total_b[...] = part[outer, :, half:]
    line_end(*line_b, total_b)
    bx_send[...] = total_b[1 - inner].astype(BF16)
    bx = pltpu.make_async_remote_copy(
        src_ref=bx_send, dst_ref=bx_recv, send_sem=bx_ss, recv_sem=bx_rs,
        device_id={"exp": neighbour}, device_id_type=MESH,
    )
    bx.start()

    for k in range(1, lanes):
        peer = at_lane(k)
        pltpu.make_async_remote_copy(
            src_ref=term_send.at[peer], dst_ref=term_recv.at[peer],
            send_sem=term_ss.at[k], recv_sem=term_rs.at[k],
            device_id={"exp": peer}, device_id_type=MESH,
        ).wait_recv()
    own_hits = own_hits_ref[...]
    own_rank = jnp.dot(own_hits.astype(BF16), before, preferred_element_type=F32) - 1.0
    spread = []
    for e in range(window):
        block = ((own_hits[e:e + 1] > 0.0) & (own_rank[e:e + 1] == slot_iota)).astype(F32)
        spread += [block, block]
    spread = jnp.transpose(jnp.concatenate(spread, axis=0)).astype(BF16)
    latent_out[...] = jnp.dot(
        spread, term_recv[...].reshape(lanes * SLOTS, term_recv.shape[2]), preferred_element_type=F32
    ).astype(BF16)

    total_a[...] = part[outer, inner, :half]
    line_end(*line_a, total_a)
    rwg_out[:half] = total_a[...]
    bx.wait_recv()
    rwg_out[half:] = total_b[inner] + bx_recv[...].astype(F32)

    def sent(src_outer, carry):
        for which in range(2):
            forward(which, src_outer, lambda c: c.wait_send())
        chain(src_outer, lambda c: c.wait_send())
        return carry

    lax.fori_loop(0, outers, sent, 0)
    for k in range(1, lanes):
        pick_copy(k).wait_send()
        gate_copy(at_lane(k)).wait_send()
        term_copy(k).wait_send()
    for k in range(1, toks):
        band_copy(k).wait_send()
    for d in range(outers):
        ax_copy(d).wait_send()
    line_sent(*line_b)
    line_sent(*line_a)
    bx.wait_send()
    for k in range(toks // 2):
        logit_copy(True, k).wait_send()
        if k:
            logit_copy(False, k).wait_send()


def hand_over(*refs):
    count = len(refs) // 2
    sems = refs[-1]
    copies = [
        pltpu.make_async_copy(refs[k], refs[count + k], sems.at[k]) for k in range(count)
    ]
    for copy in copies:
        copy.start()
    for copy in copies:
        copy.wait()


def shards(
    x_tokens, router_weight, gate_rest, latent_in, latent_grad, expert_picks, expert_in, expert_out
):
    toks = lax.axis_size("tok")
    lanes = lax.axis_size("exp")
    rows, width = x_tokens.shape
    experts = router_weight.shape[1]
    window = experts - gate_rest.shape[1]
    latent, hidden = expert_in.shape[1:]
    feats = width // toks
    own_rows = feats // lanes
    outers = lanes // 2
    half = own_rows // 2
    pad = -(-window // 8) * 8
    vmem = pl.BlockSpec(memory_space=pltpu.VMEM)
    anywhere = pl.BlockSpec(memory_space=pl.ANY)
    dma = pltpu.SemaphoreType.DMA
    results = pl.pallas_call(
        functools.partial(kernel, toks, lanes, window),
        out_shape=(
            jax.ShapeDtypeStruct((rows, latent), BF16),
            jax.ShapeDtypeStruct((rows, width), BF16),
            jax.ShapeDtypeStruct((own_rows, experts), F32),
        ),
        in_specs=[vmem] * 5 + [anywhere] * 3,
        out_specs=(vmem, vmem, vmem),
        scratch_shapes=[
            pltpu.VMEM((width, experts), BF16),
            pltpu.VMEM((hidden, latent), BF16),
            pltpu.VMEM((hidden, latent), BF16),
            pltpu.VMEM((2, lanes, rows, latent), BF16),
            pltpu.VMEM((rows, experts), F32),
            pltpu.VMEM((lanes, pad, rows), F32),
            pltpu.VMEM((pad, rows), F32),
            pltpu.VMEM((lanes, 8, rows), F32),
            pltpu.VMEM((lanes, 8, rows), F32),
            pltpu.VMEM((128, rows), F32),
            pltpu.VMEM((rows, experts), F32),
            pltpu.VMEM((lanes, rows), F32),
            pltpu.VMEM((pad, rows), F32),
            pltpu.VMEM((lanes, rows), F32),
            pltpu.VMEM((lanes, SLOTS, hidden), BF16),
            pltpu.VMEM((lanes, SLOTS, latent), BF16),
            pltpu.VMEM((lanes, SLOTS, latent), BF16),
            pltpu.VMEM((toks, rows, feats), BF16),
            pltpu.VMEM((feats, toks * rows), BF16),
            pltpu.VMEM((toks, rows, experts), BF16),
            pltpu.VMEM((outers, 2, own_rows, experts), F32),
            pltpu.VMEM((outers, half, experts), BF16),
            pltpu.VMEM((outers, half, experts), BF16),
            pltpu.VMEM((2, outers, 2, half, experts), BF16),
            pltpu.VMEM((2, outers, 2, half, experts), BF16),
            pltpu.VMEM((half, experts), BF16),
            pltpu.VMEM((half, experts), BF16),
            pltpu.VMEM((2, outers, half, experts), BF16),
            pltpu.VMEM((2, outers, half, experts), BF16),
            pltpu.VMEM((half, experts), F32),
            pltpu.VMEM((2, half, experts), F32),
            dma((3,)),
            dma((3, 2, outers)),
            dma((2,)),
            dma((2, outers)),
            dma((2, outers)),
            dma((lanes,)), dma((lanes,)),
            dma((lanes,)), dma((lanes,)),
            dma((lanes,)), dma((lanes,)),
            dma((toks,)), dma((toks,)),
            dma((toks,)), dma((toks,)),
            dma((outers,)), dma((outers,)),
            dma((2, outers)), dma((2, outers)),
            dma, dma,
            dma((2, outers)), dma((2, outers)),
        ],
        compiler_params=pltpu.CompilerParams(
            collective_id=0, has_side_effects=True, vmem_limit_bytes=56 * 1024 * 1024
        ),
    )(
        x_tokens, gate_rest, latent_in, latent_grad, expert_picks.T, router_weight,
        jnp.swapaxes(expert_in, 1, 2), expert_out,
    )
    return pl.pallas_call(
        hand_over,
        out_shape=tuple(jax.ShapeDtypeStruct(r.shape, r.dtype) for r in results),
        in_specs=[anywhere] * len(results),
        out_specs=(anywhere,) * len(results),
        scratch_shapes=[dma((len(results),))],
    )(*results)


def solution(mesh):
    placed = (
        P(("tok", "exp"), None),
        P(),
        P(("tok", "exp"), None),
        P(("tok", "exp"), None),
        P(("tok", "exp"), None),
        P("tok", None),
        P("exp", None, None),
        P("exp", None, None),
    )
    return jax.shard_map(
        shards,
        mesh=mesh,
        in_specs=placed,
        out_specs=(P(("tok", "exp"), None), P(("tok", "exp"), None), P(("tok", "exp"), None)),
        check_vma=False,
    )
```

```python
import functools
import jax
import jax.numpy as jnp
from jax import lax
from jax.experimental import pallas as pl
from jax.experimental.pallas import tpu as pltpu
from jax.sharding import PartitionSpec as P

MESH = pl.DeviceIdType.MESH
F32 = jnp.float32
BF16 = jnp.bfloat16
NT = (((1,), (1,)), ((), ()))
SLOTS = 16


def kernel(
    toks, lanes, window,
    x_ref, gate_ref, latin_ref, latgrad_ref, picks_ref, rw_hbm, win_hbm, wout_hbm,
    latent_out, xgrad_out, rwg_out,
    rw, win, wout, lat, probs, pick_recv, pick_send, gate_recv, gate_send, gate_rows, gate_grads, hits_ref, own_hits_ref, rank, packed, active_ref,
    term_send, term_recv, xband, xturned, logits_all, part, ax_send, ax_recv,
    bz_send, bz_recv, bx_send, bx_recv, az_send, az_recv, total_a, total_b,
    load_sem, send_lat, chain_ss, recv_z, recv_x, pick_ss, pick_rs, gate_ss, gate_rs, term_ss, term_rs,
    band_ss, band_rs, log_ss, log_rs, ax_ss, ax_rs, bz_ss, bz_rs, bx_ss, bx_rs,
    az_ss, az_rs,
):
    tok = lax.axis_index("tok")
    lane = lax.axis_index("exp")
    outers = lanes // 2
    outer = lane // 2
    inner = lane % 2
    expert = lane // 2
    rows = x_ref.shape[0]
    feats = x_ref.shape[1] // toks
    half = feats // lanes // 2

    loads = [
        pltpu.make_async_copy(rw_hbm, rw, load_sem.at[0]),
        pltpu.make_async_copy(win_hbm.at[0], win, load_sem.at[1]),
        pltpu.make_async_copy(wout_hbm.at[0], wout, load_sem.at[2]),
    ]
    for load in loads:
        load.start()

    def at_lane(k):
        return lax.rem(lane + k, lanes)

    def at_tok(k):
        return lax.rem(tok + k, toks)

    barrier = pltpu.get_barrier_semaphore()
    for k in range(1, lanes):
        pl.semaphore_signal(barrier, inc=1, device_id={"exp": at_lane(k)}, device_id_type=MESH)
    for k in range(1, toks):
        pl.semaphore_signal(barrier, inc=1, device_id={"tok": at_tok(k)}, device_id_type=MESH)
    lat[0, lane] = latin_ref[...]
    lat[1, lane] = latgrad_ref[...]
    pl.semaphore_wait(barrier, lanes - 1 + toks - 1)

    def lat_copy(kind, which, src_outer, src_inner):
        slot = src_outer * 2 + src_inner
        if kind == 2:
            peer, recv = outer * 2 + 1 - inner, recv_x.at[which, src_outer]
        else:
            peer, recv = lane + (2 if kind == 0 else -2), recv_z.at[which, src_outer]
        return pltpu.make_async_remote_copy(
            src_ref=lat.at[which, slot], dst_ref=lat.at[which, slot],
            send_sem=send_lat.at[kind, which, src_outer], recv_sem=recv,
            device_id={"exp": peer}, device_id_type=MESH,
        )

    def forward(which, src_outer, do):
        @pl.when((src_outer <= outer) & (outer < outers - 1))
        def _():
            do(lat_copy(0, which, src_outer, inner))

        @pl.when((src_outer >= outer) & (outer > 0))
        def _():
            do(lat_copy(1, which, src_outer, inner))

        if which == 0:
            do(lat_copy(2, which, src_outer, inner))
        else:
            @pl.when((src_outer == outer) | ((src_outer > 0) & (src_outer < outers - 1)))
            def _():
                do(lat_copy(2, which, src_outer, inner))

    def chain(src_outer, do):
        slot = src_outer * 2 + 1 - inner
        for side, end in ((1, 0), (-1, outers - 1)):
            @pl.when((src_outer == end) & (outer + side >= 0) & (outer + side < outers))
            def _():
                do(pltpu.make_async_remote_copy(
                    src_ref=lat.at[1, slot], dst_ref=lat.at[1, slot],
                    send_sem=chain_ss.at[0 if side == 1 else 1], recv_sem=recv_x.at[1, src_outer],
                    device_id={"exp": lane + 2 * side}, device_id_type=MESH,
                ))

    for which in range(2):
        forward(which, outer, lambda c: c.start())

    def band_copy(k):
        peer = at_tok(k)
        return pltpu.make_async_remote_copy(
            src_ref=x_ref.at[:, pl.ds(pl.multiple_of(peer * feats, 128), feats)],
            dst_ref=xband.at[tok],
            send_sem=band_ss.at[k], recv_sem=band_rs.at[toks - k],
            device_id={"tok": peer}, device_id_type=MESH,
        )

    for k in range(1, toks):
        band_copy(k).start()
    xband[tok] = x_ref[:, pl.ds(pl.multiple_of(tok * feats, 128), feats)]

    def any_row(picks, e):
        return jnp.max((picks == e).astype(F32), axis=0, keepdims=True)

    group_hits = any_row(picks_ref[...], expert)
    for k in range(lanes):
        hits_ref[k:k + 1, :] = group_hits[:, k * rows:(k + 1) * rows]
    own_picks = picks_ref[:, pl.ds(pl.multiple_of(lane * rows, rows), rows)]
    own_hits_ref[...] = jnp.zeros_like(own_hits_ref)
    for e in range(window):
        own_hits_ref[e:e + 1, :] = any_row(own_picks, e)
    rest = gate_ref.shape[1]
    gate_grads[:, rest - rest % 128:] = jnp.zeros_like(gate_grads[:, rest - rest % 128:])
    gate_grads[:, :rest] = gate_ref[...]
    gate_grads[...] = pltpu.roll(gate_grads[...], window, 1)

    loads[0].wait()
    logits = jnp.dot(x_ref[...], rw[...], preferred_element_type=F32)
    shifted = jnp.exp(logits - jnp.max(logits, axis=1, keepdims=True))
    probs[...] = shifted / jnp.sum(shifted, axis=1, keepdims=True)
    pad = own_hits_ref.shape[0]
    pick_send[...] = jnp.transpose(probs[:, :128])[:pad] * own_hits_ref[...]
    pick_recv[0] = pick_send[...]

    def pick_copy(k):
        return pltpu.make_async_remote_copy(
            src_ref=pick_send, dst_ref=pick_recv.at[lanes - k],
            send_sem=pick_ss.at[k], recv_sem=pick_rs.at[lanes - k],
            device_id={"exp": at_lane(k)}, device_id_type=MESH,
        )

    for k in range(1, lanes):
        pick_copy(k).start()
    before = (
        lax.broadcasted_iota(jnp.int32, (rows, rows), 0)
        <= lax.broadcasted_iota(jnp.int32, (rows, rows), 1)
    ).astype(BF16)
    rank[...] = jnp.dot(hits_ref[...].astype(BF16), before, preferred_element_type=F32) - 1.0
    slot_iota = lax.broadcasted_iota(jnp.int32, (SLOTS, rows), 0).astype(F32)
    loads[1].wait()
    loads[2].wait()
    for k in range(1, lanes):
        pick_copy(k).wait_recv()

    def gate_copy(src_lane):
        return pltpu.make_async_remote_copy(
            src_ref=gate_send.at[src_lane], dst_ref=gate_recv.at[lane],
            send_sem=gate_ss.at[src_lane], recv_sem=gate_rs.at[lane],
            device_id={"exp": src_lane}, device_id_type=MESH,
        )

    def pair_rows(src_outer, wait_for):
        first = src_outer * 2
        both = lat.shape[3]
        wait_for(0)
        rows_in = lat[0, pl.ds(first, 2)].reshape(2 * rows, both)
        active_ref[...] = jnp.maximum(lax.dot_general(rows_in, win[...], NT, preferred_element_type=F32), 0.0)
        wait_for(1)
        rows_grad = lat[1, pl.ds(first, 2)].reshape(2 * rows, both)
        grad = lax.dot_general(rows_grad, wout[...], NT, preferred_element_type=F32)
        active = active_ref[...]
        product = active * grad
        gate = jnp.sum(active * product, axis=1, keepdims=True)
        gate_row = jnp.transpose(jnp.broadcast_to(gate, (2 * rows, 128)))[:8]
        for side in range(2):
            gate_send[first + side] = gate_row[:, side * rows:(side + 1) * rows]

            @pl.when(first + side == lane)
            def _():
                gate_recv[lane] = gate_row[:, side * rows:(side + 1) * rows]

            @pl.when(first + side != lane)
            def _():
                gate_copy(first + side).start()

        raw_rows = (2.0 * product).astype(BF16)
        for side in range(2):
            src_lane = first + side
            chosen = (
                (hits_ref[pl.ds(src_lane, 1), :] > 0.0) & (rank[pl.ds(src_lane, 1), :] == slot_iota)
            ).astype(F32)
            picked = pick_recv[lax.rem(src_lane - lane + lanes, lanes), pl.ds(expert, 1), :]
            scale = jnp.sum(chosen * picked, axis=1, keepdims=True)
            raw = jnp.dot(
                chosen.astype(BF16), raw_rows[side * rows:(side + 1) * rows], preferred_element_type=F32
            )
            packed[src_lane] = (raw * scale).astype(BF16)

    def arrivals(step, carry):
        for side in (-1, 1):
            src_outer = outer + side * step

            @pl.when((step > 0) & (step < outers) & (src_outer >= 0) & (src_outer < outers))
            def _():
                for which in range(2):
                    lat_copy(0, which, src_outer, inner).wait_recv()
                    forward(which, src_outer, lambda c: c.start())

        def pair(q, carry):
            distance = step - 1
            src_outer = outer + (2 * q - 1) * distance
            valid = (src_outer >= 0) & (src_outer < outers) & (distance >= 0)
            valid = valid & ((distance > 0) | (q == 0))

            @pl.when(valid)
            def _():
                def wait_for(which):
                    lat_copy(2, which, src_outer, 1 - inner).wait_recv()
                    if which == 1:
                        chain(src_outer, lambda c: c.start())

                pair_rows(src_outer, wait_for)

            return carry

        lax.fori_loop(0, 2, pair, 0)

        @pl.when(step == outers - 1)
        def _():
            for k in range(toks):
                if k:
                    band_copy(k).wait_recv()
            for k in range(toks):
                xturned[:, k * rows:(k + 1) * rows] = jnp.transpose(xband[k])

        return carry

    lax.fori_loop(0, outers + 1, arrivals, 0)

    for k in range(1, lanes):
        peer = at_lane(k)
        pltpu.make_async_remote_copy(
            src_ref=gate_send.at[peer], dst_ref=gate_recv.at[peer],
            send_sem=gate_ss.at[peer], recv_sem=gate_rs.at[peer],
            device_id={"exp": peer}, device_id_type=MESH,
        ).wait_recv()
    gate_rows[...] = jnp.zeros_like(gate_rows)
    for e in range(window):
        gate_rows[e:e + 1, :] = gate_recv[2 * e, 0:1, :] + gate_recv[2 * e + 1, 0:1, :]
    gate_grads[:, :128] = gate_grads[:, :128] + jnp.transpose(gate_rows[...])
    gate_grad = gate_grads[...]
    prob = probs[...]
    centre = jnp.sum(prob * gate_grad, axis=1, keepdims=True)
    logit_low = (prob * (gate_grad - centre)).astype(BF16)
    logits_all[tok] = logit_low
    sibling = tok + 1 - 2 * lax.rem(tok, 2)

    def logit_copy(to_sibling, k):
        far = lax.rem(tok + 2 * k, toks)
        src = far if to_sibling else tok
        sem = (toks // 2 + k) if to_sibling else (toks // 2 - k) % (toks // 2)
        return pltpu.make_async_remote_copy(
            src_ref=logits_all.at[src], dst_ref=logits_all.at[src],
            send_sem=log_ss.at[toks // 2 + k if to_sibling else k], recv_sem=log_rs.at[sem],
            device_id={"tok": sibling if to_sibling else far}, device_id_type=MESH,
        )

    for k in range(1, toks // 2):
        logit_copy(False, k).start()
    logit_copy(True, 0).start()

    terms = jnp.dot(
        packed[...].reshape(lanes * SLOTS, packed.shape[2]), win[...], preferred_element_type=F32
    )
    term_send[...] = terms.astype(BF16).reshape(term_send.shape)

    def term_copy(k):
        return pltpu.make_async_remote_copy(
            src_ref=term_send.at[at_lane(k)], dst_ref=term_recv.at[lane],
            send_sem=term_ss.at[k], recv_sem=term_rs.at[lanes - k],
            device_id={"exp": at_lane(k)}, device_id_type=MESH,
        )

    for k in range(1, lanes):
        term_copy(k).start()
    term_recv[lane] = term_send[lane]

    for k in range(toks // 2 - 1, 0, -1):
        logit_copy(False, toks // 2 - k).wait_recv()
        logit_copy(True, k).start()
    for k in range(toks // 2):
        logit_copy(True, k).wait_recv()

    experts = rw.shape[1]
    part[...] = jnp.dot(
        xturned[...], logits_all[...].reshape(toks * rows, experts), preferred_element_type=F32
    ).reshape(part.shape)
    neighbour = outer * 2 + 1 - inner

    def ax_copy(d):
        return pltpu.make_async_remote_copy(
            src_ref=ax_send.at[d], dst_ref=ax_recv.at[d], send_sem=ax_ss.at[d], recv_sem=ax_rs.at[d],
            device_id={"exp": neighbour}, device_id_type=MESH,
        )

    for d in range(outers):
        ax_send[d] = part[d, 1 - inner, :half].astype(BF16)
        ax_copy(d).start()

    def line_copy(send, recv, ss, rs, way, side, d):
        return pltpu.make_async_remote_copy(
            src_ref=send.at[way, d], dst_ref=recv.at[way, d], send_sem=ss.at[way, d],
            recv_sem=rs.at[way, d], device_id={"exp": lane + 2 * side}, device_id_type=MESH,
        )

    def line_item(m):
        j, q = m // 2, m % 2
        side = (1 - 2 * ((outer * 2) // outers)) * (1 - 2 * q)
        d = ((side + 1) // 2) * (outers - 1 - 2 * j) + j
        return (1 - side) // 2, side, d

    def line(send, recv, ss, rs, own):
        def item(m, carry):
            way, side, d = line_item(m)
            ahead = (d - outer) * side > 0
            behind = (outer - side >= 0) & (outer - side < outers)

            @pl.when(ahead & behind)
            def _():
                line_copy(send, recv, ss, rs, way, side, d).wait_recv()
                send[way, d] = (own(d) + recv[way, d].astype(F32)).astype(BF16)

            @pl.when(ahead & jnp.logical_not(behind))
            def _():
                send[way, d] = own(d).astype(BF16)

            @pl.when(ahead)
            def _():
                line_copy(send, recv, ss, rs, way, side, d).start()

            return carry

        lax.fori_loop(0, 2 * outers, item, 0)

    def line_end(send, recv, ss, rs, total):
        for way, side in ((0, 1), (1, -1)):
            @pl.when((outer - side >= 0) & (outer - side < outers))
            def _():
                line_copy(send, recv, ss, rs, way, side, outer).wait_recv()
                total[...] = total[...] + recv[way, outer].astype(F32)

    def line_sent(send, recv, ss, rs):
        def item(m, carry):
            way, side, d = line_item(m)

            @pl.when((d - outer) * side > 0)
            def _():
                line_copy(send, recv, ss, rs, way, side, d).wait_send()

            return carry

        lax.fori_loop(0, 2 * outers, item, 0)

    line_b = (bz_send, bz_recv, bz_ss, bz_rs)
    line_a = (az_send, az_recv, az_ss, az_rs)
    line(*line_b, lambda d: part[d, :, half:])
    for d in range(outers):
        ax_copy(d).wait_recv()
        part[d, inner, :half] = part[d, inner, :half] + ax_recv[d].astype(F32)
    line(*line_a, lambda d: part[d, inner, :half])
    total_b[...] = part[outer, :, half:]
    line_end(*line_b, total_b)
    bx_send[...] = total_b[1 - inner].astype(BF16)
    bx = pltpu.make_async_remote_copy(
        src_ref=bx_send, dst_ref=bx_recv, send_sem=bx_ss, recv_sem=bx_rs,
        device_id={"exp": neighbour}, device_id_type=MESH,
    )
    bx.start()

    for k in range(1, lanes):
        peer = at_lane(k)
        pltpu.make_async_remote_copy(
            src_ref=term_send.at[peer], dst_ref=term_recv.at[peer],
            send_sem=term_ss.at[k], recv_sem=term_rs.at[k],
            device_id={"exp": peer}, device_id_type=MESH,
        ).wait_recv()
    own_hits = own_hits_ref[...]
    own_rank = jnp.dot(own_hits.astype(BF16), before, preferred_element_type=F32) - 1.0
    spread = []
    for e in range(window):
        block = ((own_hits[e:e + 1] > 0.0) & (own_rank[e:e + 1] == slot_iota)).astype(F32)
        spread += [block, block]
    spread = jnp.transpose(jnp.concatenate(spread, axis=0)).astype(BF16)
    latent_out[...] = jnp.dot(
        spread, term_recv[...].reshape(lanes * SLOTS, term_recv.shape[2]), preferred_element_type=F32
    ).astype(BF16)

    xgrad_out[...] = lax.dot_general(logit_low, rw[...], NT, preferred_element_type=F32).astype(BF16)

    total_a[...] = part[outer, inner, :half]
    line_end(*line_a, total_a)
    rwg_out[:half] = total_a[...]
    bx.wait_recv()
    rwg_out[half:] = total_b[inner] + bx_recv[...].astype(F32)

    def sent(src_outer, carry):
        for which in range(2):
            forward(which, src_outer, lambda c: c.wait_send())
        chain(src_outer, lambda c: c.wait_send())
        return carry

    lax.fori_loop(0, outers, sent, 0)
    for k in range(1, lanes):
        pick_copy(k).wait_send()
        gate_copy(at_lane(k)).wait_send()
        term_copy(k).wait_send()
    for k in range(1, toks):
        band_copy(k).wait_send()
    for d in range(outers):
        ax_copy(d).wait_send()
    line_sent(*line_b)
    line_sent(*line_a)
    bx.wait_send()
    for k in range(toks // 2):
        logit_copy(True, k).wait_send()
        if k:
            logit_copy(False, k).wait_send()


def hand_over(*refs):
    count = len(refs) // 3
    sems = refs[-1]
    ins, outs, held = refs[:count], refs[count:2 * count], refs[2 * count:3 * count]
    loads = [pltpu.make_async_copy(ins[k], held[k], sems.at[k]) for k in range(count)]
    stores = [pltpu.make_async_copy(held[k], outs[k], sems.at[count + k]) for k in range(count)]
    for load in loads:
        load.start()
    for load, store in zip(loads, stores):
        load.wait()
        store.start()
    for store in stores:
        store.wait()


def shards(
    x_tokens, router_weight, gate_rest, latent_in, latent_grad, expert_picks, expert_in, expert_out
):
    toks = lax.axis_size("tok")
    lanes = lax.axis_size("exp")
    rows, width = x_tokens.shape
    experts = router_weight.shape[1]
    window = experts - gate_rest.shape[1]
    latent, hidden = expert_in.shape[1:]
    feats = width // toks
    own_rows = feats // lanes
    outers = lanes // 2
    half = own_rows // 2
    pad = -(-window // 8) * 8
    vmem = pl.BlockSpec(memory_space=pltpu.VMEM)
    anywhere = pl.BlockSpec(memory_space=pl.ANY)
    dma = pltpu.SemaphoreType.DMA
    results = pl.pallas_call(
        functools.partial(kernel, toks, lanes, window),
        out_shape=(
            jax.ShapeDtypeStruct((rows, latent), BF16),
            jax.ShapeDtypeStruct((rows, width), BF16),
            jax.ShapeDtypeStruct((own_rows, experts), F32),
        ),
        in_specs=[vmem] * 5 + [anywhere] * 3,
        out_specs=(vmem, vmem, vmem),
        scratch_shapes=[
            pltpu.VMEM((width, experts), BF16),
            pltpu.VMEM((hidden, latent), BF16),
            pltpu.VMEM((hidden, latent), BF16),
            pltpu.VMEM((2, lanes, rows, latent), BF16),
            pltpu.VMEM((rows, experts), F32),
            pltpu.VMEM((lanes, pad, rows), F32),
            pltpu.VMEM((pad, rows), F32),
            pltpu.VMEM((lanes, 8, rows), F32),
            pltpu.VMEM((lanes, 8, rows), F32),
            pltpu.VMEM((128, rows), F32),
            pltpu.VMEM((rows, experts), F32),
            pltpu.VMEM((lanes, rows), F32),
            pltpu.VMEM((pad, rows), F32),
            pltpu.VMEM((lanes, rows), F32),
            pltpu.VMEM((lanes, SLOTS, hidden), BF16),
            pltpu.VMEM((2 * rows, hidden), F32),
            pltpu.VMEM((lanes, SLOTS, latent), BF16),
            pltpu.VMEM((lanes, SLOTS, latent), BF16),
            pltpu.VMEM((toks, rows, feats), BF16),
            pltpu.VMEM((feats, toks * rows), BF16),
            pltpu.VMEM((toks, rows, experts), BF16),
            pltpu.VMEM((outers, 2, own_rows, experts), F32),
            pltpu.VMEM((outers, half, experts), BF16),
            pltpu.VMEM((outers, half, experts), BF16),
            pltpu.VMEM((2, outers, 2, half, experts), BF16),
            pltpu.VMEM((2, outers, 2, half, experts), BF16),
            pltpu.VMEM((half, experts), BF16),
            pltpu.VMEM((half, experts), BF16),
            pltpu.VMEM((2, outers, half, experts), BF16),
            pltpu.VMEM((2, outers, half, experts), BF16),
            pltpu.VMEM((half, experts), F32),
            pltpu.VMEM((2, half, experts), F32),
            dma((3,)),
            dma((3, 2, outers)),
            dma((2,)),
            dma((2, outers)),
            dma((2, outers)),
            dma((lanes,)), dma((lanes,)),
            dma((lanes,)), dma((lanes,)),
            dma((lanes,)), dma((lanes,)),
            dma((toks,)), dma((toks,)),
            dma((toks,)), dma((toks,)),
            dma((outers,)), dma((outers,)),
            dma((2, outers)), dma((2, outers)),
            dma, dma,
            dma((2, outers)), dma((2, outers)),
        ],
        compiler_params=pltpu.CompilerParams(
            collective_id=0, has_side_effects=True, vmem_limit_bytes=56 * 1024 * 1024
        ),
    )(
        x_tokens, gate_rest, latent_in, latent_grad, expert_picks.T, router_weight,
        jnp.swapaxes(expert_in, 1, 2), expert_out,
    )
    return pl.pallas_call(
        hand_over,
        out_shape=tuple(jax.ShapeDtypeStruct(r.shape, r.dtype) for r in results),
        in_specs=[anywhere] * len(results),
        out_specs=(anywhere,) * len(results),
        scratch_shapes=[pltpu.VMEM(r.shape, r.dtype) for r in results] + [dma((2 * len(results),))],
    )(*results)


def solution(mesh):
    placed = (
        P(("tok", "exp"), None),
        P(),
        P(("tok", "exp"), None),
        P(("tok", "exp"), None),
        P(("tok", "exp"), None),
        P("tok", None),
        P("exp", None, None),
        P("exp", None, None),
    )
    return jax.shard_map(
        shards,
        mesh=mesh,
        in_specs=placed,
        out_specs=(P(("tok", "exp"), None), P(("tok", "exp"), None), P(("tok", "exp"), None)),
        check_vma=False,
    )
```

```python
import functools
import jax
import jax.numpy as jnp
from jax import lax
from jax.experimental import pallas as pl
from jax.experimental.pallas import tpu as pltpu
from jax.sharding import PartitionSpec as P

MESH = pl.DeviceIdType.MESH
F32 = jnp.float32
BF16 = jnp.bfloat16
NT = (((1,), (1,)), ((), ()))
SLOTS = 16


def kernel(
    toks, lanes, window,
    x_hbm, gate_hbm, latin_hbm, latgrad_hbm, picks_hbm, rw_hbm, win_hbm, wout_hbm,
    latent_hbm, xgrad_hbm, rwg_out,
    x_ref, gate_ref, picks_ref, latent_out, xgrad_out,
    rw, win, wout, lat, probs, pick_recv, pick_send, gate_recv, gate_send, gate_rows, gate_grads, hits_ref, own_hits_ref, rank, packed, active_ref,
    term_send, term_recv, xband, xturned, logits_all, part, ax_send, ax_recv,
    bz_send, bz_recv, bx_send, bx_recv, az_send, az_recv, total_a, total_b,
    load_sem, send_lat, chain_ss, recv_z, recv_x, pick_ss, pick_rs, gate_ss, gate_rs, term_ss, term_rs,
    band_ss, band_rs, log_ss, log_rs, ax_ss, ax_rs, bz_ss, bz_rs, bx_ss, bx_rs,
    az_ss, az_rs,
):
    tok = lax.axis_index("tok")
    lane = lax.axis_index("exp")
    outers = lanes // 2
    outer = lane // 2
    inner = lane % 2
    expert = lane // 2
    rows = x_ref.shape[0]
    own_rows = rwg_out.shape[0]
    feats = x_ref.shape[1] // toks
    half = ax_send.shape[1]

    first_loads = [
        pltpu.make_async_copy(latin_hbm, lat.at[0, lane], load_sem.at[3]),
        pltpu.make_async_copy(latgrad_hbm, lat.at[1, lane], load_sem.at[4]),
        pltpu.make_async_copy(x_hbm, x_ref, load_sem.at[5]),
        pltpu.make_async_copy(picks_hbm, picks_ref, load_sem.at[6]),
        pltpu.make_async_copy(gate_hbm, gate_ref, load_sem.at[7]),
    ]
    loads = [
        pltpu.make_async_copy(rw_hbm, rw, load_sem.at[0]),
        pltpu.make_async_copy(win_hbm.at[0], win, load_sem.at[1]),
        pltpu.make_async_copy(wout_hbm.at[0], wout, load_sem.at[2]),
    ]
    stores = [
        pltpu.make_async_copy(latent_out, latent_hbm, load_sem.at[8]),
        pltpu.make_async_copy(xgrad_out, xgrad_hbm, load_sem.at[9]),
    ]
    for load in first_loads + loads:
        load.start()

    def at_lane(k):
        return lax.rem(lane + k, lanes)

    def at_tok(k):
        return lax.rem(tok + k, toks)

    barrier = pltpu.get_barrier_semaphore()
    for k in range(1, lanes):
        pl.semaphore_signal(barrier, inc=1, device_id={"exp": at_lane(k)}, device_id_type=MESH)
    for k in range(1, toks):
        pl.semaphore_signal(barrier, inc=1, device_id={"tok": at_tok(k)}, device_id_type=MESH)
    first_loads[0].wait()
    first_loads[1].wait()
    pl.semaphore_wait(barrier, lanes - 1 + toks - 1)

    def lat_copy(kind, which, src_outer, src_inner):
        slot = src_outer * 2 + src_inner
        if kind == 2:
            peer, recv = outer * 2 + 1 - inner, recv_x.at[which, src_outer]
        else:
            peer, recv = lane + (2 if kind == 0 else -2), recv_z.at[which, src_outer]
        return pltpu.make_async_remote_copy(
            src_ref=lat.at[which, slot], dst_ref=lat.at[which, slot],
            send_sem=send_lat.at[kind, which, src_outer], recv_sem=recv,
            device_id={"exp": peer}, device_id_type=MESH,
        )

    def forward(which, src_outer, do):
        @pl.when((src_outer <= outer) & (outer < outers - 1))
        def _():
            do(lat_copy(0, which, src_outer, inner))

        @pl.when((src_outer >= outer) & (outer > 0))
        def _():
            do(lat_copy(1, which, src_outer, inner))

        if which == 0:
            do(lat_copy(2, which, src_outer, inner))
        else:
            @pl.when((src_outer == outer) | ((src_outer > 0) & (src_outer < outers - 1)))
            def _():
                do(lat_copy(2, which, src_outer, inner))

    def chain(src_outer, do):
        slot = src_outer * 2 + 1 - inner
        for side, end in ((1, 0), (-1, outers - 1)):
            @pl.when((src_outer == end) & (outer + side >= 0) & (outer + side < outers))
            def _():
                do(pltpu.make_async_remote_copy(
                    src_ref=lat.at[1, slot], dst_ref=lat.at[1, slot],
                    send_sem=chain_ss.at[0 if side == 1 else 1], recv_sem=recv_x.at[1, src_outer],
                    device_id={"exp": lane + 2 * side}, device_id_type=MESH,
                ))

    for which in range(2):
        forward(which, outer, lambda c: c.start())

    def band_copy(k):
        peer = at_tok(k)
        return pltpu.make_async_remote_copy(
            src_ref=x_ref.at[:, pl.ds(pl.multiple_of(peer * feats, 128), feats)],
            dst_ref=xband.at[tok],
            send_sem=band_ss.at[k], recv_sem=band_rs.at[toks - k],
            device_id={"tok": peer}, device_id_type=MESH,
        )

    for load in first_loads[2:]:
        load.wait()
    for k in range(1, toks):
        band_copy(k).start()
    xband[tok] = x_ref[:, pl.ds(pl.multiple_of(tok * feats, 128), feats)]

    def any_row(picks, e):
        return jnp.max((picks == e).astype(F32), axis=0, keepdims=True)

    group_hits = any_row(picks_ref[...], expert)
    for k in range(lanes):
        hits_ref[k:k + 1, :] = group_hits[:, k * rows:(k + 1) * rows]
    own_picks = picks_ref[:, pl.ds(pl.multiple_of(lane * rows, rows), rows)]
    own_hits_ref[...] = jnp.zeros_like(own_hits_ref)
    for e in range(window):
        own_hits_ref[e:e + 1, :] = any_row(own_picks, e)
    rest = gate_ref.shape[1]
    gate_grads[:, rest - rest % 128:] = jnp.zeros_like(gate_grads[:, rest - rest % 128:])
    gate_grads[:, :rest] = gate_ref[...]
    gate_grads[...] = pltpu.roll(gate_grads[...], window, 1)

    loads[0].wait()
    logits = jnp.dot(x_ref[...], rw[...], preferred_element_type=F32)
    shifted = jnp.exp(logits - jnp.max(logits, axis=1, keepdims=True))
    probs[...] = shifted / jnp.sum(shifted, axis=1, keepdims=True)
    pad = own_hits_ref.shape[0]
    pick_send[...] = jnp.transpose(probs[:, :128])[:pad] * own_hits_ref[...]
    pick_recv[0] = pick_send[...]

    def pick_copy(k):
        return pltpu.make_async_remote_copy(
            src_ref=pick_send, dst_ref=pick_recv.at[lanes - k],
            send_sem=pick_ss.at[k], recv_sem=pick_rs.at[lanes - k],
            device_id={"exp": at_lane(k)}, device_id_type=MESH,
        )

    for k in range(1, lanes):
        pick_copy(k).start()
    before = (
        lax.broadcasted_iota(jnp.int32, (rows, rows), 0)
        <= lax.broadcasted_iota(jnp.int32, (rows, rows), 1)
    ).astype(BF16)
    rank[...] = jnp.dot(hits_ref[...].astype(BF16), before, preferred_element_type=F32) - 1.0
    slot_iota = lax.broadcasted_iota(jnp.int32, (SLOTS, rows), 0).astype(F32)
    loads[1].wait()
    loads[2].wait()
    for k in range(1, lanes):
        pick_copy(k).wait_recv()

    def gate_copy(src_lane):
        return pltpu.make_async_remote_copy(
            src_ref=gate_send.at[src_lane], dst_ref=gate_recv.at[lane],
            send_sem=gate_ss.at[src_lane], recv_sem=gate_rs.at[lane],
            device_id={"exp": src_lane}, device_id_type=MESH,
        )

    def pair_rows(src_outer, wait_for):
        first = src_outer * 2
        both = lat.shape[3]
        wait_for(0)
        rows_in = lat[0, pl.ds(first, 2)].reshape(2 * rows, both)
        active_ref[...] = jnp.maximum(lax.dot_general(rows_in, win[...], NT, preferred_element_type=F32), 0.0)
        wait_for(1)
        rows_grad = lat[1, pl.ds(first, 2)].reshape(2 * rows, both)
        grad = lax.dot_general(rows_grad, wout[...], NT, preferred_element_type=F32)
        active = active_ref[...]
        product = active * grad
        gate = jnp.sum(active * product, axis=1, keepdims=True)
        gate_row = jnp.transpose(jnp.broadcast_to(gate, (2 * rows, 128)))[:8]
        for side in range(2):
            gate_send[first + side] = gate_row[:, side * rows:(side + 1) * rows]

            @pl.when(first + side == lane)
            def _():
                gate_recv[lane] = gate_row[:, side * rows:(side + 1) * rows]

            @pl.when(first + side != lane)
            def _():
                gate_copy(first + side).start()

        raw_rows = (2.0 * product).astype(BF16)
        for side in range(2):
            src_lane = first + side
            chosen = (
                (hits_ref[pl.ds(src_lane, 1), :] > 0.0) & (rank[pl.ds(src_lane, 1), :] == slot_iota)
            ).astype(F32)
            picked = pick_recv[lax.rem(src_lane - lane + lanes, lanes), pl.ds(expert, 1), :]
            scale = jnp.sum(chosen * picked, axis=1, keepdims=True)
            raw = jnp.dot(
                chosen.astype(BF16), raw_rows[side * rows:(side + 1) * rows], preferred_element_type=F32
            )
            packed[src_lane] = (raw * scale).astype(BF16)

    def arrivals(step, carry):
        for side in (-1, 1):
            src_outer = outer + side * step

            @pl.when((step > 0) & (step < outers) & (src_outer >= 0) & (src_outer < outers))
            def _():
                for which in range(2):
                    lat_copy(0, which, src_outer, inner).wait_recv()
                    forward(which, src_outer, lambda c: c.start())

        for side in (-1, 1):
            far = outer + side * (step - 1)

            @pl.when((step > 0) & ((step > 1) | (side == 1)) & ((far == 0) | (far == outers - 1)))
            def _():
                lat_copy(2, 1, far, 1 - inner).wait_recv()
                chain(far, lambda c: c.start())

        def pair(q, carry):
            distance = step - 1
            src_outer = outer + (2 * q - 1) * distance
            valid = (src_outer >= 0) & (src_outer < outers) & (distance >= 0)
            valid = valid & ((distance > 0) | (q == 0))

            @pl.when(valid)
            def _():
                def wait_for(which):
                    if which == 0:
                        lat_copy(2, which, src_outer, 1 - inner).wait_recv()
                    else:
                        @pl.when((src_outer > 0) & (src_outer < outers - 1))
                        def _():
                            lat_copy(2, which, src_outer, 1 - inner).wait_recv()

                pair_rows(src_outer, wait_for)

            return carry

        lax.fori_loop(0, 2, pair, 0)

        @pl.when(step == outers - 1)
        def _():
            for k in range(toks):
                if k:
                    band_copy(k).wait_recv()
            for k in range(toks):
                xturned[:, k * rows:(k + 1) * rows] = jnp.transpose(xband[k])

        return carry

    lax.fori_loop(0, outers + 1, arrivals, 0)

    for k in range(1, lanes):
        peer = at_lane(k)
        pltpu.make_async_remote_copy(
            src_ref=gate_send.at[peer], dst_ref=gate_recv.at[peer],
            send_sem=gate_ss.at[peer], recv_sem=gate_rs.at[peer],
            device_id={"exp": peer}, device_id_type=MESH,
        ).wait_recv()
    gate_rows[...] = jnp.zeros_like(gate_rows)
    for e in range(window):
        gate_rows[e:e + 1, :] = gate_recv[2 * e, 0:1, :] + gate_recv[2 * e + 1, 0:1, :]
    gate_grads[:, :128] = gate_grads[:, :128] + jnp.transpose(gate_rows[...])
    gate_grad = gate_grads[...]
    prob = probs[...]
    centre = jnp.sum(prob * gate_grad, axis=1, keepdims=True)
    logit_low = (prob * (gate_grad - centre)).astype(BF16)
    logits_all[tok] = logit_low
    sibling = tok + 1 - 2 * lax.rem(tok, 2)

    def logit_copy(to_sibling, k):
        far = lax.rem(tok + 2 * k, toks)
        src = far if to_sibling else tok
        sem = (toks // 2 + k) if to_sibling else (toks // 2 - k) % (toks // 2)
        return pltpu.make_async_remote_copy(
            src_ref=logits_all.at[src], dst_ref=logits_all.at[src],
            send_sem=log_ss.at[toks // 2 + k if to_sibling else k], recv_sem=log_rs.at[sem],
            device_id={"tok": sibling if to_sibling else far}, device_id_type=MESH,
        )

    for k in range(1, toks // 2):
        logit_copy(False, k).start()
    logit_copy(True, 0).start()

    terms = jnp.dot(
        packed[...].reshape(lanes * SLOTS, packed.shape[2]), win[...], preferred_element_type=F32
    )
    term_send[...] = terms.astype(BF16).reshape(term_send.shape)

    def term_copy(k):
        return pltpu.make_async_remote_copy(
            src_ref=term_send.at[at_lane(k)], dst_ref=term_recv.at[lane],
            send_sem=term_ss.at[k], recv_sem=term_rs.at[lanes - k],
            device_id={"exp": at_lane(k)}, device_id_type=MESH,
        )

    for k in range(1, lanes):
        term_copy(k).start()
    term_recv[lane] = term_send[lane]

    for k in range(toks // 2 - 1, 0, -1):
        logit_copy(False, toks // 2 - k).wait_recv()
        logit_copy(True, k).start()
    for k in range(toks // 2):
        logit_copy(True, k).wait_recv()

    experts = rw.shape[1]
    part[...] = jnp.dot(
        xturned[...], logits_all[...].reshape(toks * rows, experts), preferred_element_type=F32
    ).reshape(part.shape)
    neighbour = outer * 2 + 1 - inner

    def ax_copy(d):
        return pltpu.make_async_remote_copy(
            src_ref=ax_send.at[d], dst_ref=ax_recv.at[d], send_sem=ax_ss.at[d], recv_sem=ax_rs.at[d],
            device_id={"exp": neighbour}, device_id_type=MESH,
        )

    def line_copy(send, recv, ss, rs, way, side, d):
        return pltpu.make_async_remote_copy(
            src_ref=send.at[way, d], dst_ref=recv.at[way, d], send_sem=ss.at[way, d],
            recv_sem=rs.at[way, d], device_id={"exp": lane + 2 * side}, device_id_type=MESH,
        )

    def line_item(m):
        j, q = m // 2, m % 2
        side = (1 - 2 * ((outer * 2) // outers)) * (1 - 2 * q)
        d = ((side + 1) // 2) * (outers - 1 - 2 * j) + j
        return (1 - side) // 2, side, d

    def ax_start(m, carry):
        way, side, d = line_item(m)

        @pl.when((d - outer) * side > 0)
        def _():
            ax_send[d] = part[d, 1 - inner, :half].astype(BF16)
            ax_copy(d).start()

        return carry

    lax.fori_loop(0, 2 * outers, ax_start, 0)
    ax_send[outer] = part[outer, 1 - inner, :half].astype(BF16)
    ax_copy(outer).start()

    def ax_wait(d):
        ax_copy(d).wait_recv()
        part[d, inner, :half] = part[d, inner, :half] + ax_recv[d].astype(F32)

    def line(send, recv, ss, rs, own, ready):
        def item(m, carry):
            way, side, d = line_item(m)
            ahead = (d - outer) * side > 0
            behind = (outer - side >= 0) & (outer - side < outers)

            @pl.when(ahead)
            def _():
                ready(d)

            @pl.when(ahead & behind)
            def _():
                line_copy(send, recv, ss, rs, way, side, d).wait_recv()
                send[way, d] = (own(d) + recv[way, d].astype(F32)).astype(BF16)

            @pl.when(ahead & jnp.logical_not(behind))
            def _():
                send[way, d] = own(d).astype(BF16)

            @pl.when(ahead)
            def _():
                line_copy(send, recv, ss, rs, way, side, d).start()

            return carry

        lax.fori_loop(0, 2 * outers, item, 0)

    def line_end(send, recv, ss, rs, total):
        for way, side in ((0, 1), (1, -1)):
            @pl.when((outer - side >= 0) & (outer - side < outers))
            def _():
                line_copy(send, recv, ss, rs, way, side, outer).wait_recv()
                total[...] = total[...] + recv[way, outer].astype(F32)

    def line_sent(send, recv, ss, rs):
        def item(m, carry):
            way, side, d = line_item(m)

            @pl.when((d - outer) * side > 0)
            def _():
                line_copy(send, recv, ss, rs, way, side, d).wait_send()

            return carry

        lax.fori_loop(0, 2 * outers, item, 0)

    line_b = (bz_send, bz_recv, bz_ss, bz_rs)
    line_a = (az_send, az_recv, az_ss, az_rs)
    line(*line_b, lambda d: part[d, :, half:], lambda d: None)
    line(*line_a, lambda d: part[d, inner, :half], ax_wait)
    total_b[...] = part[outer, :, half:]
    line_end(*line_b, total_b)
    bx_send[...] = total_b[1 - inner].astype(BF16)
    bx = pltpu.make_async_remote_copy(
        src_ref=bx_send, dst_ref=bx_recv, send_sem=bx_ss, recv_sem=bx_rs,
        device_id={"exp": neighbour}, device_id_type=MESH,
    )
    bx.start()

    for k in range(1, lanes):
        peer = at_lane(k)
        pltpu.make_async_remote_copy(
            src_ref=term_send.at[peer], dst_ref=term_recv.at[peer],
            send_sem=term_ss.at[k], recv_sem=term_rs.at[k],
            device_id={"exp": peer}, device_id_type=MESH,
        ).wait_recv()
    own_hits = own_hits_ref[...]
    own_rank = jnp.dot(own_hits.astype(BF16), before, preferred_element_type=F32) - 1.0
    spread = []
    for e in range(window):
        block = ((own_hits[e:e + 1] > 0.0) & (own_rank[e:e + 1] == slot_iota)).astype(F32)
        spread += [block, block]
    spread = jnp.transpose(jnp.concatenate(spread, axis=0)).astype(BF16)
    latent_out[...] = jnp.dot(
        spread, term_recv[...].reshape(lanes * SLOTS, term_recv.shape[2]), preferred_element_type=F32
    ).astype(BF16)

    stores[0].start()
    xgrad_out[...] = lax.dot_general(logit_low, rw[...], NT, preferred_element_type=F32).astype(BF16)
    stores[1].start()

    ax_wait(outer)
    total_a[...] = part[outer, inner, :half]
    line_end(*line_a, total_a)
    rwg_out[:half] = total_a[...]
    bx.wait_recv()
    rwg_out[half:] = total_b[inner] + bx_recv[...].astype(F32)

    for store in stores:
        store.wait()
    def sent(src_outer, carry):
        for which in range(2):
            forward(which, src_outer, lambda c: c.wait_send())
        chain(src_outer, lambda c: c.wait_send())
        return carry

    lax.fori_loop(0, outers, sent, 0)
    for k in range(1, lanes):
        pick_copy(k).wait_send()
        gate_copy(at_lane(k)).wait_send()
        term_copy(k).wait_send()
    for k in range(1, toks):
        band_copy(k).wait_send()
    for d in range(outers):
        ax_copy(d).wait_send()
    line_sent(*line_b)
    line_sent(*line_a)
    bx.wait_send()
    for k in range(toks // 2):
        logit_copy(True, k).wait_send()
        if k:
            logit_copy(False, k).wait_send()


def hand_over(*refs):
    count = len(refs) // 3
    sems = refs[-1]
    ins, outs, held = refs[:count], refs[count:2 * count], refs[2 * count:3 * count]
    loads = [pltpu.make_async_copy(ins[k], held[k], sems.at[k]) for k in range(count)]
    stores = [pltpu.make_async_copy(held[k], outs[k], sems.at[count + k]) for k in range(count)]
    for load in loads:
        load.start()
    for load, store in zip(loads, stores):
        load.wait()
        store.start()
    for store in stores:
        store.wait()


def shards(
    x_tokens, router_weight, gate_rest, latent_in, latent_grad, expert_picks, expert_in, expert_out
):
    toks = lax.axis_size("tok")
    lanes = lax.axis_size("exp")
    rows, width = x_tokens.shape
    experts = router_weight.shape[1]
    window = experts - gate_rest.shape[1]
    latent, hidden = expert_in.shape[1:]
    feats = width // toks
    own_rows = feats // lanes
    outers = lanes // 2
    half = max(16, own_rows * 3 // 4 // 16 * 16)
    tail = own_rows - half
    pad = -(-window // 8) * 8
    vmem = pl.BlockSpec(memory_space=pltpu.VMEM)
    anywhere = pl.BlockSpec(memory_space=pl.ANY)
    dma = pltpu.SemaphoreType.DMA
    results = pl.pallas_call(
        functools.partial(kernel, toks, lanes, window),
        out_shape=(
            jax.ShapeDtypeStruct((rows, latent), BF16),
            jax.ShapeDtypeStruct((rows, width), BF16),
            jax.ShapeDtypeStruct((own_rows, experts), F32),
        ),
        in_specs=[anywhere] * 8,
        out_specs=(anywhere, anywhere, vmem),
        scratch_shapes=[
            pltpu.VMEM((rows, width), BF16),
            pltpu.VMEM(gate_rest.shape, F32),
            pltpu.VMEM((expert_picks.shape[1], expert_picks.shape[0]), jnp.int32),
            pltpu.VMEM((rows, latent), BF16),
            pltpu.VMEM((rows, width), BF16),
            pltpu.VMEM((width, experts), BF16),
            pltpu.VMEM((hidden, latent), BF16),
            pltpu.VMEM((hidden, latent), BF16),
            pltpu.VMEM((2, lanes, rows, latent), BF16),
            pltpu.VMEM((rows, experts), F32),
            pltpu.VMEM((lanes, pad, rows), F32),
            pltpu.VMEM((pad, rows), F32),
            pltpu.VMEM((lanes, 8, rows), F32),
            pltpu.VMEM((lanes, 8, rows), F32),
            pltpu.VMEM((128, rows), F32),
            pltpu.VMEM((rows, experts), F32),
            pltpu.VMEM((lanes, rows), F32),
            pltpu.VMEM((pad, rows), F32),
            pltpu.VMEM((lanes, rows), F32),
            pltpu.VMEM((lanes, SLOTS, hidden), BF16),
            pltpu.VMEM((2 * rows, hidden), F32),
            pltpu.VMEM((lanes, SLOTS, latent), BF16),
            pltpu.VMEM((lanes, SLOTS, latent), BF16),
            pltpu.VMEM((toks, rows, feats), BF16),
            pltpu.VMEM((feats, toks * rows), BF16),
            pltpu.VMEM((toks, rows, experts), BF16),
            pltpu.VMEM((outers, 2, own_rows, experts), F32),
            pltpu.VMEM((outers, half, experts), BF16),
            pltpu.VMEM((outers, half, experts), BF16),
            pltpu.VMEM((2, outers, 2, tail, experts), BF16),
            pltpu.VMEM((2, outers, 2, tail, experts), BF16),
            pltpu.VMEM((tail, experts), BF16),
            pltpu.VMEM((tail, experts), BF16),
            pltpu.VMEM((2, outers, half, experts), BF16),
            pltpu.VMEM((2, outers, half, experts), BF16),
            pltpu.VMEM((half, experts), F32),
            pltpu.VMEM((2, tail, experts), F32),
            dma((10,)),
            dma((3, 2, outers)),
            dma((2,)),
            dma((2, outers)),
            dma((2, outers)),
            dma((lanes,)), dma((lanes,)),
            dma((lanes,)), dma((lanes,)),
            dma((lanes,)), dma((lanes,)),
            dma((toks,)), dma((toks,)),
            dma((toks,)), dma((toks,)),
            dma((outers,)), dma((outers,)),
            dma((2, outers)), dma((2, outers)),
            dma, dma,
            dma((2, outers)), dma((2, outers)),
        ],
        compiler_params=pltpu.CompilerParams(
            collective_id=0, has_side_effects=True, vmem_limit_bytes=56 * 1024 * 1024
        ),
    )(
        x_tokens, gate_rest, latent_in, latent_grad, expert_picks.T, router_weight,
        jnp.swapaxes(expert_in, 1, 2), expert_out,
    )
    return pl.pallas_call(
        hand_over,
        out_shape=tuple(jax.ShapeDtypeStruct(r.shape, r.dtype) for r in results),
        in_specs=[anywhere] * len(results),
        out_specs=(anywhere,) * len(results),
        scratch_shapes=[pltpu.VMEM(r.shape, r.dtype) for r in results] + [dma((2 * len(results),))],
    )(*results)


def solution(mesh):
    placed = (
        P(("tok", "exp"), None),
        P(),
        P(("tok", "exp"), None),
        P(("tok", "exp"), None),
        P(("tok", "exp"), None),
        P("tok", None),
        P("exp", None, None),
        P("exp", None, None),
    )
    return jax.shard_map(
        shards,
        mesh=mesh,
        in_specs=placed,
        out_specs=(P(("tok", "exp"), None), P(("tok", "exp"), None), P(("tok", "exp"), None)),
        check_vma=False,
    )
```

```python
import functools
import jax
import jax.numpy as jnp
from jax import lax
from jax.experimental import pallas as pl
from jax.experimental.pallas import tpu as pltpu
from jax.sharding import PartitionSpec as P

MESH = pl.DeviceIdType.MESH
F32 = jnp.float32
BF16 = jnp.bfloat16
NT = (((1,), (1,)), ((), ()))
SLOTS = 16


def kernel(
    toks, lanes, window,
    x_hbm, gate_hbm, latin_hbm, latgrad_hbm, picks_hbm, rw_hbm, win_hbm, wout_hbm,
    latent_hbm, xgrad_hbm, rwg_out,
    x_ref, gate_ref, picks_ref, latent_out, xgrad_out,
    rw, win, wout, lat, held_all, pick_recv, pick_send, gate_recv, gate_send, gate_rows, rows_recv, gate_grads, hits_ref, own_hits_ref, rank, packed, active_ref,
    term_send, term_recv, xband, xturned, logits_all, part, ax_send, ax_recv,
    bz_send, bz_recv, bx_send, bx_recv, az_send, az_recv, total_a, total_b,
    load_sem, send_lat, chain_ss, recv_z, recv_x, pick_ss, pick_rs, gate_ss, gate_rs, term_ss, term_rs,
    band_ss, band_rs, log_ss, log_rs, held_ss, held_rs, ax_ss, ax_rs, bz_ss, bz_rs, bx_ss, bx_rs,
    az_ss, az_rs,
):
    tok = lax.axis_index("tok")
    lane = lax.axis_index("exp")
    outers = lanes // 2
    outer = lane // 2
    inner = lane % 2
    expert = lane // 2
    rows = x_ref.shape[0]
    own_rows = rwg_out.shape[0]
    feats = x_ref.shape[1] // toks
    half = ax_send.shape[1]

    first_loads = [
        pltpu.make_async_copy(latin_hbm, lat.at[0, lane], load_sem.at[3]),
        pltpu.make_async_copy(latgrad_hbm, lat.at[1, lane], load_sem.at[4]),
        pltpu.make_async_copy(x_hbm, x_ref, load_sem.at[5]),
        pltpu.make_async_copy(picks_hbm, picks_ref, load_sem.at[6]),
        pltpu.make_async_copy(gate_hbm, gate_ref, load_sem.at[7]),
    ]
    loads = [
        pltpu.make_async_copy(rw_hbm, rw, load_sem.at[0]),
        pltpu.make_async_copy(win_hbm.at[0], win, load_sem.at[1]),
        pltpu.make_async_copy(wout_hbm.at[0], wout, load_sem.at[2]),
    ]
    stores = [
        pltpu.make_async_copy(latent_out, latent_hbm, load_sem.at[8]),
        pltpu.make_async_copy(xgrad_out, xgrad_hbm, load_sem.at[9]),
    ]
    for load in first_loads + loads:
        load.start()

    def at_lane(k):
        return lax.rem(lane + k, lanes)

    def at_tok(k):
        return lax.rem(tok + k, toks)

    barrier = pltpu.get_barrier_semaphore()
    for k in range(1, lanes):
        pl.semaphore_signal(barrier, inc=1, device_id={"exp": at_lane(k)}, device_id_type=MESH)
    for k in range(1, toks):
        pl.semaphore_signal(barrier, inc=1, device_id={"tok": at_tok(k)}, device_id_type=MESH)
    first_loads[0].wait()
    first_loads[1].wait()
    pl.semaphore_wait(barrier, lanes - 1 + toks - 1)

    def lat_copy(kind, which, src_outer, src_inner):
        slot = src_outer * 2 + src_inner
        if kind == 2:
            peer, recv = outer * 2 + 1 - inner, recv_x.at[which, src_outer]
        else:
            peer, recv = lane + (2 if kind == 0 else -2), recv_z.at[which, src_outer]
        return pltpu.make_async_remote_copy(
            src_ref=lat.at[which, slot], dst_ref=lat.at[which, slot],
            send_sem=send_lat.at[kind, which, src_outer], recv_sem=recv,
            device_id={"exp": peer}, device_id_type=MESH,
        )

    def forward(which, src_outer, do):
        @pl.when((src_outer <= outer) & (outer < outers - 1))
        def _():
            do(lat_copy(0, which, src_outer, inner))

        @pl.when((src_outer >= outer) & (outer > 0))
        def _():
            do(lat_copy(1, which, src_outer, inner))

        if which == 0:
            do(lat_copy(2, which, src_outer, inner))
        else:
            @pl.when((src_outer == outer) | ((src_outer > 0) & (src_outer < outers - 1)))
            def _():
                do(lat_copy(2, which, src_outer, inner))

    def chain(src_outer, do):
        slot = src_outer * 2 + 1 - inner
        for side, end in ((1, 0), (-1, outers - 1)):
            @pl.when((src_outer == end) & (outer + side >= 0) & (outer + side < outers))
            def _():
                do(pltpu.make_async_remote_copy(
                    src_ref=lat.at[1, slot], dst_ref=lat.at[1, slot],
                    send_sem=chain_ss.at[0 if side == 1 else 1], recv_sem=recv_x.at[1, src_outer],
                    device_id={"exp": lane + 2 * side}, device_id_type=MESH,
                ))

    for which in range(2):
        forward(which, outer, lambda c: c.start())

    def band_copy(k):
        peer = at_tok(k)
        return pltpu.make_async_remote_copy(
            src_ref=x_ref.at[:, pl.ds(pl.multiple_of(peer * feats, 128), feats)],
            dst_ref=xband.at[tok],
            send_sem=band_ss.at[k], recv_sem=band_rs.at[toks - k],
            device_id={"tok": peer}, device_id_type=MESH,
        )

    for load in first_loads[2:]:
        load.wait()
    for k in range(1, toks):
        band_copy(k).start()
    xband[tok] = x_ref[:, pl.ds(pl.multiple_of(tok * feats, 128), feats)]

    def any_row(picks, e):
        return jnp.max((picks == e).astype(F32), axis=0, keepdims=True)

    group_hits = any_row(picks_ref[...], expert)
    for k in range(lanes):
        hits_ref[k:k + 1, :] = group_hits[:, k * rows:(k + 1) * rows]
    own_picks = picks_ref[:, pl.ds(pl.multiple_of(lane * rows, rows), rows)]
    own_hits_ref[...] = jnp.zeros_like(own_hits_ref)
    for e in range(window):
        own_hits_ref[e:e + 1, :] = any_row(own_picks, e)
    rest = gate_ref.shape[1]
    gate_grads[:, rest - rest % 128:] = jnp.zeros_like(gate_grads[:, rest - rest % 128:])
    gate_grads[:, :rest] = gate_ref[...]
    held_all[1, tok] = pltpu.roll(gate_grads[...], window, 1)
    sibling = tok + 1 - 2 * lax.rem(tok, 2)

    def held_copy(which, to_sibling, k):
        far = lax.rem(tok + 2 * k, toks)
        src = far if to_sibling else tok
        sem = (toks // 2 + k) if to_sibling else (toks // 2 - k) % (toks // 2)
        return pltpu.make_async_remote_copy(
            src_ref=held_all.at[which, src], dst_ref=held_all.at[which, src],
            send_sem=held_ss.at[which, toks // 2 + k if to_sibling else k], recv_sem=held_rs.at[which, sem],
            device_id={"tok": sibling if to_sibling else far}, device_id_type=MESH,
        )

    def held_start(which):
        for k in range(1, toks // 2):
            held_copy(which, False, k).start()
        held_copy(which, True, 0).start()

    held_start(1)

    loads[0].wait()
    logits = jnp.dot(x_ref[...], rw[...], preferred_element_type=F32)
    shifted = jnp.exp(logits - jnp.max(logits, axis=1, keepdims=True))
    held_all[0, tok] = shifted / jnp.sum(shifted, axis=1, keepdims=True)
    pad = own_hits_ref.shape[0]
    pick_send[...] = jnp.transpose(held_all[0, tok, :, :128])[:pad] * own_hits_ref[...]
    pick_recv[0] = pick_send[...]

    def pick_copy(k):
        return pltpu.make_async_remote_copy(
            src_ref=pick_send, dst_ref=pick_recv.at[lanes - k],
            send_sem=pick_ss.at[k], recv_sem=pick_rs.at[lanes - k],
            device_id={"exp": at_lane(k)}, device_id_type=MESH,
        )

    for k in range(1, lanes):
        pick_copy(k).start()
    held_start(0)
    before = (
        lax.broadcasted_iota(jnp.int32, (rows, rows), 0)
        <= lax.broadcasted_iota(jnp.int32, (rows, rows), 1)
    ).astype(BF16)
    rank[...] = jnp.dot(hits_ref[...].astype(BF16), before, preferred_element_type=F32) - 1.0
    slot_iota = lax.broadcasted_iota(jnp.int32, (SLOTS, rows), 0).astype(F32)
    loads[1].wait()
    loads[2].wait()
    for k in range(1, lanes):
        pick_copy(k).wait_recv()

    def gate_copy(src_lane):
        return pltpu.make_async_remote_copy(
            src_ref=gate_send.at[src_lane], dst_ref=gate_recv.at[lane],
            send_sem=gate_ss.at[src_lane], recv_sem=gate_rs.at[lane],
            device_id={"exp": src_lane}, device_id_type=MESH,
        )

    def pair_rows(src_outer, wait_for):
        first = src_outer * 2
        both = lat.shape[3]
        wait_for(0)
        rows_in = lat[0, pl.ds(first, 2)].reshape(2 * rows, both)
        active_ref[...] = jnp.maximum(lax.dot_general(rows_in, win[...], NT, preferred_element_type=F32), 0.0)
        wait_for(1)
        rows_grad = lat[1, pl.ds(first, 2)].reshape(2 * rows, both)
        grad = lax.dot_general(rows_grad, wout[...], NT, preferred_element_type=F32)
        active = active_ref[...]
        product = active * grad
        gate = jnp.sum(active * product, axis=1, keepdims=True)
        gate_row = jnp.transpose(jnp.broadcast_to(gate, (2 * rows, 128)))[:8]
        for side in range(2):
            gate_send[first + side] = gate_row[:, side * rows:(side + 1) * rows]

            @pl.when(first + side == lane)
            def _():
                gate_recv[lane] = gate_row[:, side * rows:(side + 1) * rows]

            @pl.when(first + side != lane)
            def _():
                gate_copy(first + side).start()

        raw_rows = (2.0 * product).astype(BF16)
        for side in range(2):
            src_lane = first + side
            chosen = (
                (hits_ref[pl.ds(src_lane, 1), :] > 0.0) & (rank[pl.ds(src_lane, 1), :] == slot_iota)
            ).astype(F32)
            picked = pick_recv[lax.rem(src_lane - lane + lanes, lanes), pl.ds(expert, 1), :]
            scale = jnp.sum(chosen * picked, axis=1, keepdims=True)
            raw = jnp.dot(
                chosen.astype(BF16), raw_rows[side * rows:(side + 1) * rows], preferred_element_type=F32
            )
            packed[src_lane] = (raw * scale).astype(BF16)

    def arrivals(step, carry):
        for side in (-1, 1):
            src_outer = outer + side * step

            @pl.when((step > 0) & (step < outers) & (src_outer >= 0) & (src_outer < outers))
            def _():
                for which in range(2):
                    lat_copy(0, which, src_outer, inner).wait_recv()
                    forward(which, src_outer, lambda c: c.start())

        for side in (-1, 1):
            far = outer + side * (step - 1)

            @pl.when((step > 0) & ((step > 1) | (side == 1)) & ((far == 0) | (far == outers - 1)))
            def _():
                lat_copy(2, 1, far, 1 - inner).wait_recv()
                chain(far, lambda c: c.start())

        def pair(q, carry):
            distance = step - 1
            src_outer = outer + (2 * q - 1) * distance
            valid = (src_outer >= 0) & (src_outer < outers) & (distance >= 0)
            valid = valid & ((distance > 0) | (q == 0))

            @pl.when(valid)
            def _():
                def wait_for(which):
                    if which == 0:
                        lat_copy(2, which, src_outer, 1 - inner).wait_recv()
                    else:
                        @pl.when((src_outer > 0) & (src_outer < outers - 1))
                        def _():
                            lat_copy(2, which, src_outer, 1 - inner).wait_recv()

                pair_rows(src_outer, wait_for)

            return carry

        lax.fori_loop(0, 2, pair, 0)

        @pl.when(step == outers - 1)
        def _():
            for which in range(2):
                for k in range(toks // 2 - 1, 0, -1):
                    held_copy(which, False, toks // 2 - k).wait_recv()
                    held_copy(which, True, k).start()
            for k in range(toks):
                if k:
                    band_copy(k).wait_recv()
            for k in range(toks):
                xturned[:, k * rows:(k + 1) * rows] = jnp.transpose(xband[k])

        return carry

    lax.fori_loop(0, outers + 1, arrivals, 0)

    for k in range(1, lanes):
        peer = at_lane(k)
        pltpu.make_async_remote_copy(
            src_ref=gate_send.at[peer], dst_ref=gate_recv.at[peer],
            send_sem=gate_ss.at[peer], recv_sem=gate_rs.at[peer],
            device_id={"exp": peer}, device_id_type=MESH,
        ).wait_recv()
    gate_rows[...] = jnp.zeros_like(gate_rows)
    for e in range(window):
        gate_rows[tok, e:e + 1, :] = gate_recv[2 * e, 0:1, :] + gate_recv[2 * e + 1, 0:1, :]

    def row_copy(k):
        return pltpu.make_async_remote_copy(
            src_ref=gate_rows.at[tok, pl.ds(0, pad)], dst_ref=rows_recv.at[tok],
            send_sem=log_ss.at[k], recv_sem=log_rs.at[toks - k],
            device_id={"tok": at_tok(k)}, device_id_type=MESH,
        )

    for k in range(1, toks):
        row_copy(k).start()

    def logit_rows(t):
        head = held_all[1, t, :, :128] + jnp.transpose(gate_rows[t])
        gate_grad = jnp.concatenate([head, held_all[1, t, :, 128:]], axis=1)
        prob = held_all[0, t]
        centre = jnp.sum(prob * gate_grad, axis=1, keepdims=True)
        logits_all[t] = (prob * (gate_grad - centre)).astype(BF16)

    logit_rows(tok)

    terms = jnp.dot(
        packed[...].reshape(lanes * SLOTS, packed.shape[2]), win[...], preferred_element_type=F32
    )
    term_send[...] = terms.astype(BF16).reshape(term_send.shape)

    def term_copy(k):
        return pltpu.make_async_remote_copy(
            src_ref=term_send.at[at_lane(k)], dst_ref=term_recv.at[lane],
            send_sem=term_ss.at[k], recv_sem=term_rs.at[lanes - k],
            device_id={"exp": at_lane(k)}, device_id_type=MESH,
        )

    for k in range(1, lanes):
        term_copy(k).start()
    term_recv[lane] = term_send[lane]

    for which in range(2):
        for k in range(toks // 2):
            held_copy(which, True, k).wait_recv()
    for k in range(1, toks):
        peer = at_tok(k)
        pltpu.make_async_remote_copy(
            src_ref=gate_rows.at[tok, pl.ds(0, pad)], dst_ref=rows_recv.at[peer],
            send_sem=log_ss.at[k], recv_sem=log_rs.at[k],
            device_id={"tok": peer}, device_id_type=MESH,
        ).wait_recv()
        gate_rows[peer, :pad] = rows_recv[peer]
        logit_rows(peer)

    experts = rw.shape[1]
    part[...] = jnp.dot(
        xturned[...], logits_all[...].reshape(toks * rows, experts), preferred_element_type=F32
    ).reshape(part.shape)
    neighbour = outer * 2 + 1 - inner

    def ax_copy(d):
        return pltpu.make_async_remote_copy(
            src_ref=ax_send.at[d], dst_ref=ax_recv.at[d], send_sem=ax_ss.at[d], recv_sem=ax_rs.at[d],
            device_id={"exp": neighbour}, device_id_type=MESH,
        )

    def line_copy(send, recv, ss, rs, way, side, d):
        return pltpu.make_async_remote_copy(
            src_ref=send.at[way, d], dst_ref=recv.at[way, d], send_sem=ss.at[way, d],
            recv_sem=rs.at[way, d], device_id={"exp": lane + 2 * side}, device_id_type=MESH,
        )

    def line_item(m):
        j, q = m // 2, m % 2
        side = (1 - 2 * ((outer * 2) // outers)) * (1 - 2 * q)
        d = ((side + 1) // 2) * (outers - 1 - 2 * j) + j
        return (1 - side) // 2, side, d

    def ax_start(m, carry):
        way, side, d = line_item(m)

        @pl.when((d - outer) * side > 0)
        def _():
            ax_send[d] = part[d, 1 - inner, :half].astype(BF16)
            ax_copy(d).start()

        return carry

    lax.fori_loop(0, 2 * outers, ax_start, 0)
    ax_send[outer] = part[outer, 1 - inner, :half].astype(BF16)
    ax_copy(outer).start()

    def ax_wait(d):
        ax_copy(d).wait_recv()
        part[d, inner, :half] = part[d, inner, :half] + ax_recv[d].astype(F32)

    def line(send, recv, ss, rs, own, ready):
        def item(m, carry):
            way, side, d = line_item(m)
            ahead = (d - outer) * side > 0
            behind = (outer - side >= 0) & (outer - side < outers)

            @pl.when(ahead)
            def _():
                ready(d)

            @pl.when(ahead & behind)
            def _():
                line_copy(send, recv, ss, rs, way, side, d).wait_recv()
                send[way, d] = (own(d) + recv[way, d].astype(F32)).astype(BF16)

            @pl.when(ahead & jnp.logical_not(behind))
            def _():
                send[way, d] = own(d).astype(BF16)

            @pl.when(ahead)
            def _():
                line_copy(send, recv, ss, rs, way, side, d).start()

            return carry

        lax.fori_loop(0, 2 * outers, item, 0)

    def line_end(send, recv, ss, rs, total):
        for way, side in ((0, 1), (1, -1)):
            @pl.when((outer - side >= 0) & (outer - side < outers))
            def _():
                line_copy(send, recv, ss, rs, way, side, outer).wait_recv()
                total[...] = total[...] + recv[way, outer].astype(F32)

    def line_sent(send, recv, ss, rs):
        def item(m, carry):
            way, side, d = line_item(m)

            @pl.when((d - outer) * side > 0)
            def _():
                line_copy(send, recv, ss, rs, way, side, d).wait_send()

            return carry

        lax.fori_loop(0, 2 * outers, item, 0)

    line_b = (bz_send, bz_recv, bz_ss, bz_rs)
    line_a = (az_send, az_recv, az_ss, az_rs)
    line(*line_b, lambda d: part[d, :, half:], lambda d: None)
    line(*line_a, lambda d: part[d, inner, :half], ax_wait)
    total_b[...] = part[outer, :, half:]
    line_end(*line_b, total_b)
    bx_send[...] = total_b[1 - inner].astype(BF16)
    bx = pltpu.make_async_remote_copy(
        src_ref=bx_send, dst_ref=bx_recv, send_sem=bx_ss, recv_sem=bx_rs,
        device_id={"exp": neighbour}, device_id_type=MESH,
    )
    bx.start()

    for k in range(1, lanes):
        peer = at_lane(k)
        pltpu.make_async_remote_copy(
            src_ref=term_send.at[peer], dst_ref=term_recv.at[peer],
            send_sem=term_ss.at[k], recv_sem=term_rs.at[k],
            device_id={"exp": peer}, device_id_type=MESH,
        ).wait_recv()
    own_hits = own_hits_ref[...]
    own_rank = jnp.dot(own_hits.astype(BF16), before, preferred_element_type=F32) - 1.0
    spread = []
    for e in range(window):
        block = ((own_hits[e:e + 1] > 0.0) & (own_rank[e:e + 1] == slot_iota)).astype(F32)
        spread += [block, block]
    spread = jnp.transpose(jnp.concatenate(spread, axis=0)).astype(BF16)
    latent_out[...] = jnp.dot(
        spread, term_recv[...].reshape(lanes * SLOTS, term_recv.shape[2]), preferred_element_type=F32
    ).astype(BF16)

    stores[0].start()
    xgrad_out[...] = lax.dot_general(logits_all[tok], rw[...], NT, preferred_element_type=F32).astype(BF16)
    stores[1].start()

    ax_wait(outer)
    total_a[...] = part[outer, inner, :half]
    line_end(*line_a, total_a)
    rwg_out[:half] = total_a[...]
    bx.wait_recv()
    rwg_out[half:] = total_b[inner] + bx_recv[...].astype(F32)

    for store in stores:
        store.wait()
    def sent(src_outer, carry):
        for which in range(2):
            forward(which, src_outer, lambda c: c.wait_send())
        chain(src_outer, lambda c: c.wait_send())
        return carry

    lax.fori_loop(0, outers, sent, 0)
    for k in range(1, lanes):
        pick_copy(k).wait_send()
        gate_copy(at_lane(k)).wait_send()
        term_copy(k).wait_send()
    for k in range(1, toks):
        band_copy(k).wait_send()
    for d in range(outers):
        ax_copy(d).wait_send()
    line_sent(*line_b)
    line_sent(*line_a)
    bx.wait_send()
    for k in range(1, toks):
        row_copy(k).wait_send()
    for which in range(2):
        for k in range(toks // 2):
            held_copy(which, True, k).wait_send()
            if k:
                held_copy(which, False, k).wait_send()


def hand_over(*refs):
    count = len(refs) // 3
    sems = refs[-1]
    ins, outs, held = refs[:count], refs[count:2 * count], refs[2 * count:3 * count]
    loads = [pltpu.make_async_copy(ins[k], held[k], sems.at[k]) for k in range(count)]
    stores = [pltpu.make_async_copy(held[k], outs[k], sems.at[count + k]) for k in range(count)]
    for load in loads:
        load.start()
    for load, store in zip(loads, stores):
        load.wait()
        store.start()
    for store in stores:
        store.wait()


def shards(
    x_tokens, router_weight, gate_rest, latent_in, latent_grad, expert_picks, expert_in, expert_out
):
    toks = lax.axis_size("tok")
    lanes = lax.axis_size("exp")
    rows, width = x_tokens.shape
    experts = router_weight.shape[1]
    window = experts - gate_rest.shape[1]
    latent, hidden = expert_in.shape[1:]
    feats = width // toks
    own_rows = feats // lanes
    outers = lanes // 2
    half = max(16, own_rows * 3 // 4 // 16 * 16)
    tail = own_rows - half
    pad = -(-window // 8) * 8
    vmem = pl.BlockSpec(memory_space=pltpu.VMEM)
    anywhere = pl.BlockSpec(memory_space=pl.ANY)
    dma = pltpu.SemaphoreType.DMA
    results = pl.pallas_call(
        functools.partial(kernel, toks, lanes, window),
        out_shape=(
            jax.ShapeDtypeStruct((rows, latent), BF16),
            jax.ShapeDtypeStruct((rows, width), BF16),
            jax.ShapeDtypeStruct((own_rows, experts), F32),
        ),
        in_specs=[anywhere] * 8,
        out_specs=(anywhere, anywhere, vmem),
        scratch_shapes=[
            pltpu.VMEM((rows, width), BF16),
            pltpu.VMEM(gate_rest.shape, F32),
            pltpu.VMEM((expert_picks.shape[1], expert_picks.shape[0]), jnp.int32),
            pltpu.VMEM((rows, latent), BF16),
            pltpu.VMEM((rows, width), BF16),
            pltpu.VMEM((width, experts), BF16),
            pltpu.VMEM((hidden, latent), BF16),
            pltpu.VMEM((hidden, latent), BF16),
            pltpu.VMEM((2, lanes, rows, latent), BF16),
            pltpu.VMEM((2, toks, rows, experts), F32),
            pltpu.VMEM((lanes, pad, rows), F32),
            pltpu.VMEM((pad, rows), F32),
            pltpu.VMEM((lanes, 8, rows), F32),
            pltpu.VMEM((lanes, 8, rows), F32),
            pltpu.VMEM((toks, 128, rows), F32),
            pltpu.VMEM((toks, pad, rows), F32),
            pltpu.VMEM((rows, experts), F32),
            pltpu.VMEM((lanes, rows), F32),
            pltpu.VMEM((pad, rows), F32),
            pltpu.VMEM((lanes, rows), F32),
            pltpu.VMEM((lanes, SLOTS, hidden), BF16),
            pltpu.VMEM((2 * rows, hidden), F32),
            pltpu.VMEM((lanes, SLOTS, latent), BF16),
            pltpu.VMEM((lanes, SLOTS, latent), BF16),
            pltpu.VMEM((toks, rows, feats), BF16),
            pltpu.VMEM((feats, toks * rows), BF16),
            pltpu.VMEM((toks, rows, experts), BF16),
            pltpu.VMEM((outers, 2, own_rows, experts), F32),
            pltpu.VMEM((outers, half, experts), BF16),
            pltpu.VMEM((outers, half, experts), BF16),
            pltpu.VMEM((2, outers, 2, tail, experts), BF16),
            pltpu.VMEM((2, outers, 2, tail, experts), BF16),
            pltpu.VMEM((tail, experts), BF16),
            pltpu.VMEM((tail, experts), BF16),
            pltpu.VMEM((2, outers, half, experts), BF16),
            pltpu.VMEM((2, outers, half, experts), BF16),
            pltpu.VMEM((half, experts), F32),
            pltpu.VMEM((2, tail, experts), F32),
            dma((10,)),
            dma((3, 2, outers)),
            dma((2,)),
            dma((2, outers)),
            dma((2, outers)),
            dma((lanes,)), dma((lanes,)),
            dma((lanes,)), dma((lanes,)),
            dma((lanes,)), dma((lanes,)),
            dma((toks,)), dma((toks,)),
            dma((toks,)), dma((toks,)),
            dma((2, toks)), dma((2, toks)),
            dma((outers,)), dma((outers,)),
            dma((2, outers)), dma((2, outers)),
            dma, dma,
            dma((2, outers)), dma((2, outers)),
        ],
        compiler_params=pltpu.CompilerParams(
            collective_id=0, has_side_effects=True, vmem_limit_bytes=56 * 1024 * 1024
        ),
    )(
        x_tokens, gate_rest, latent_in, latent_grad, expert_picks.T, router_weight,
        jnp.swapaxes(expert_in, 1, 2), expert_out,
    )
    return pl.pallas_call(
        hand_over,
        out_shape=tuple(jax.ShapeDtypeStruct(r.shape, r.dtype) for r in results),
        in_specs=[anywhere] * len(results),
        out_specs=(anywhere,) * len(results),
        scratch_shapes=[pltpu.VMEM(r.shape, r.dtype) for r in results] + [dma((2 * len(results),))],
    )(*results)


def solution(mesh):
    placed = (
        P(("tok", "exp"), None),
        P(),
        P(("tok", "exp"), None),
        P(("tok", "exp"), None),
        P(("tok", "exp"), None),
        P("tok", None),
        P("exp", None, None),
        P("exp", None, None),
    )
    return jax.shard_map(
        shards,
        mesh=mesh,
        in_specs=placed,
        out_specs=(P(("tok", "exp"), None), P(("tok", "exp"), None), P(("tok", "exp"), None)),
        check_vma=False,
    )
```

```python
import functools
import jax
import jax.numpy as jnp
from jax import lax
from jax.experimental import pallas as pl
from jax.experimental.pallas import tpu as pltpu
from jax.sharding import PartitionSpec as P

MESH = pl.DeviceIdType.MESH
F32 = jnp.float32
BF16 = jnp.bfloat16
NT = (((1,), (1,)), ((), ()))
SLOTS = 16


def kernel(
    toks, lanes, window,
    x_hbm, gate_hbm, latin_hbm, latgrad_hbm, picks_hbm, rw_hbm, win_hbm, wout_hbm,
    latent_hbm, xgrad_hbm, rwg_out,
    x_ref, gate_ref, picks_ref, latent_out, xgrad_out,
    rw, win, wout, lat, held_all, pick_recv, pick_send, gate_recv, gate_send, gate_rows, rows_recv, gate_grads, hits_ref, own_hits_ref, rank, packed, active_ref,
    term_send, term_recv, xband, xturned, logits_all, part, ax_send, ax_recv,
    bz_send, bz_recv, bx_send, bx_recv, az_send, az_recv, total_a, total_b,
    load_sem, send_lat, chain_ss, recv_z, recv_x, pick_ss, pick_rs, gate_ss, gate_rs, term_ss, term_rs,
    band_ss, band_rs, log_ss, log_rs, held_ss, held_rs, ax_ss, ax_rs, bz_ss, bz_rs, bx_ss, bx_rs,
    az_ss, az_rs,
):
    tok = lax.axis_index("tok")
    lane = lax.axis_index("exp")
    outers = lanes // 2
    outer = lane // 2
    inner = lane % 2
    expert = lane // 2
    rows = x_ref.shape[0]
    own_rows = rwg_out.shape[0]
    feats = x_ref.shape[1] // toks
    half = ax_send.shape[1]

    first_loads = [
        pltpu.make_async_copy(latin_hbm, lat.at[0, lane], load_sem.at[3]),
        pltpu.make_async_copy(latgrad_hbm, lat.at[1, lane], load_sem.at[4]),
        pltpu.make_async_copy(x_hbm, x_ref, load_sem.at[5]),
        pltpu.make_async_copy(picks_hbm, picks_ref, load_sem.at[6]),
        pltpu.make_async_copy(gate_hbm, gate_ref, load_sem.at[7]),
    ]
    loads = [
        pltpu.make_async_copy(rw_hbm, rw, load_sem.at[0]),
        pltpu.make_async_copy(win_hbm.at[0], win, load_sem.at[1]),
        pltpu.make_async_copy(wout_hbm.at[0], wout, load_sem.at[2]),
    ]
    stores = [
        pltpu.make_async_copy(latent_out, latent_hbm, load_sem.at[8]),
        pltpu.make_async_copy(xgrad_out, xgrad_hbm, load_sem.at[9]),
    ]
    for load in first_loads + loads:
        load.start()

    def at_lane(k):
        return lax.rem(lane + k, lanes)

    def at_tok(k):
        return lax.rem(tok + k, toks)

    barrier = pltpu.get_barrier_semaphore()
    for k in range(1, lanes):
        pl.semaphore_signal(barrier, inc=1, device_id={"exp": at_lane(k)}, device_id_type=MESH)
    for k in range(1, toks):
        pl.semaphore_signal(barrier, inc=1, device_id={"tok": at_tok(k)}, device_id_type=MESH)
    first_loads[0].wait()
    first_loads[1].wait()
    pl.semaphore_wait(barrier, lanes - 1 + toks - 1)

    def lat_copy(kind, which, src_outer, src_inner):
        slot = src_outer * 2 + src_inner
        if kind == 2:
            peer, recv = outer * 2 + 1 - inner, recv_x.at[which, src_outer]
        else:
            peer, recv = lane + (2 if kind == 0 else -2), recv_z.at[which, src_outer]
        return pltpu.make_async_remote_copy(
            src_ref=lat.at[which, slot], dst_ref=lat.at[which, slot],
            send_sem=send_lat.at[kind, which, src_outer], recv_sem=recv,
            device_id={"exp": peer}, device_id_type=MESH,
        )

    def forward(which, src_outer, do):
        @pl.when((src_outer <= outer) & (outer < outers - 1))
        def _():
            do(lat_copy(0, which, src_outer, inner))

        @pl.when((src_outer >= outer) & (outer > 0))
        def _():
            do(lat_copy(1, which, src_outer, inner))

        if which == 0:
            do(lat_copy(2, which, src_outer, inner))
        else:
            @pl.when((src_outer == outer) | ((src_outer > 0) & (src_outer < outers - 1)))
            def _():
                do(lat_copy(2, which, src_outer, inner))

    def chain(src_outer, do):
        slot = src_outer * 2 + 1 - inner
        for side, end in ((1, 0), (-1, outers - 1)):
            @pl.when((src_outer == end) & (outer + side >= 0) & (outer + side < outers))
            def _():
                do(pltpu.make_async_remote_copy(
                    src_ref=lat.at[1, slot], dst_ref=lat.at[1, slot],
                    send_sem=chain_ss.at[0 if side == 1 else 1], recv_sem=recv_x.at[1, src_outer],
                    device_id={"exp": lane + 2 * side}, device_id_type=MESH,
                ))

    for which in range(2):
        forward(which, outer, lambda c: c.start())

    def band_copy(k):
        peer = at_tok(k)
        return pltpu.make_async_remote_copy(
            src_ref=x_ref.at[:, pl.ds(pl.multiple_of(peer * feats, 128), feats)],
            dst_ref=xband.at[tok],
            send_sem=band_ss.at[k], recv_sem=band_rs.at[toks - k],
            device_id={"tok": peer}, device_id_type=MESH,
        )

    for load in first_loads[2:]:
        load.wait()
    for k in range(1, toks):
        band_copy(k).start()
    xband[tok] = x_ref[:, pl.ds(pl.multiple_of(tok * feats, 128), feats)]

    def any_row(picks, e):
        return jnp.max((picks == e).astype(F32), axis=0, keepdims=True)

    group_hits = any_row(picks_ref[...], expert)
    for k in range(lanes):
        hits_ref[k:k + 1, :] = group_hits[:, k * rows:(k + 1) * rows]
    own_picks = picks_ref[:, pl.ds(pl.multiple_of(lane * rows, rows), rows)]
    own_hits_ref[...] = jnp.zeros_like(own_hits_ref)
    for e in range(window):
        own_hits_ref[e:e + 1, :] = any_row(own_picks, e)
    rest = gate_ref.shape[1]
    gate_grads[:, rest - rest % 128:] = jnp.zeros_like(gate_grads[:, rest - rest % 128:])
    gate_grads[:, :rest] = gate_ref[...]
    held_all[1, tok] = pltpu.roll(gate_grads[...], window, 1)
    sibling = tok + 1 - 2 * lax.rem(tok, 2)

    def held_copy(which, to_sibling, k):
        far = lax.rem(tok + 2 * k, toks)
        src = far if to_sibling else tok
        sem = (toks // 2 + k) if to_sibling else (toks // 2 - k) % (toks // 2)
        return pltpu.make_async_remote_copy(
            src_ref=held_all.at[which, src], dst_ref=held_all.at[which, src],
            send_sem=held_ss.at[which, toks // 2 + k if to_sibling else k], recv_sem=held_rs.at[which, sem],
            device_id={"tok": sibling if to_sibling else far}, device_id_type=MESH,
        )

    def held_start(which):
        for k in range(1, toks // 2):
            held_copy(which, False, k).start()
        held_copy(which, True, 0).start()

    held_start(1)

    loads[0].wait()
    logits = jnp.dot(x_ref[...], rw[...], preferred_element_type=F32)
    shifted = jnp.exp(logits - jnp.max(logits, axis=1, keepdims=True))
    held_all[0, tok] = shifted / jnp.sum(shifted, axis=1, keepdims=True)
    pad = own_hits_ref.shape[0]
    pick_send[...] = jnp.transpose(held_all[0, tok, :, :128])[:pad] * own_hits_ref[...]
    pick_recv[0] = pick_send[...]

    def pick_copy(k):
        return pltpu.make_async_remote_copy(
            src_ref=pick_send, dst_ref=pick_recv.at[lanes - k],
            send_sem=pick_ss.at[k], recv_sem=pick_rs.at[lanes - k],
            device_id={"exp": at_lane(k)}, device_id_type=MESH,
        )

    for k in range(1, lanes):
        pick_copy(k).start()
    held_start(0)
    before = (
        lax.broadcasted_iota(jnp.int32, (rows, rows), 0)
        <= lax.broadcasted_iota(jnp.int32, (rows, rows), 1)
    ).astype(BF16)
    rank[...] = jnp.dot(hits_ref[...].astype(BF16), before, preferred_element_type=F32) - 1.0
    slot_iota = lax.broadcasted_iota(jnp.int32, (SLOTS, rows), 0).astype(F32)
    loads[1].wait()
    loads[2].wait()
    for k in range(1, lanes):
        pick_copy(k).wait_recv()

    def gate_copy(src_lane):
        return pltpu.make_async_remote_copy(
            src_ref=gate_send.at[src_lane], dst_ref=gate_recv.at[lane],
            send_sem=gate_ss.at[src_lane], recv_sem=gate_rs.at[lane],
            device_id={"exp": src_lane}, device_id_type=MESH,
        )

    def pair_rows(src_outer, wait_for):
        first = src_outer * 2
        both = lat.shape[3]
        wait_for(0)
        rows_in = lat[0, pl.ds(first, 2)].reshape(2 * rows, both)
        active_ref[...] = jnp.maximum(lax.dot_general(rows_in, win[...], NT, preferred_element_type=F32), 0.0)
        wait_for(1)
        rows_grad = lat[1, pl.ds(first, 2)].reshape(2 * rows, both)
        grad = lax.dot_general(rows_grad, wout[...], NT, preferred_element_type=F32)
        active = active_ref[...]
        product = active * grad
        gate = jnp.sum(active * product, axis=1, keepdims=True)
        gate_row = jnp.transpose(jnp.broadcast_to(gate, (2 * rows, 128)))[:8]
        for side in range(2):
            gate_send[first + side] = gate_row[:, side * rows:(side + 1) * rows]

            @pl.when(first + side == lane)
            def _():
                gate_recv[lane] = gate_row[:, side * rows:(side + 1) * rows]

            @pl.when(first + side != lane)
            def _():
                gate_copy(first + side).start()

        raw_rows = (2.0 * product).astype(BF16)
        for side in range(2):
            src_lane = first + side
            chosen = (
                (hits_ref[pl.ds(src_lane, 1), :] > 0.0) & (rank[pl.ds(src_lane, 1), :] == slot_iota)
            ).astype(F32)
            picked = pick_recv[lax.rem(src_lane - lane + lanes, lanes), pl.ds(expert, 1), :]
            scale = jnp.sum(chosen * picked, axis=1, keepdims=True)
            raw = jnp.dot(
                chosen.astype(BF16), raw_rows[side * rows:(side + 1) * rows], preferred_element_type=F32
            )
            packed[src_lane] = (raw * scale).astype(BF16)

    def arrivals(step, carry):
        for side in (-1, 1):
            src_outer = outer + side * step

            @pl.when((step > 0) & (step < outers) & (src_outer >= 0) & (src_outer < outers))
            def _():
                for which in range(2):
                    lat_copy(0, which, src_outer, inner).wait_recv()
                    forward(which, src_outer, lambda c: c.start())

        for side in (-1, 1):
            far = outer + side * (step - 1)

            @pl.when((step > 0) & ((step > 1) | (side == 1)) & ((far == 0) | (far == outers - 1)))
            def _():
                lat_copy(2, 1, far, 1 - inner).wait_recv()
                chain(far, lambda c: c.start())

        def pair(q, carry):
            distance = step - 1
            src_outer = outer + (2 * q - 1) * distance
            valid = (src_outer >= 0) & (src_outer < outers) & (distance >= 0)
            valid = valid & ((distance > 0) | (q == 0))

            @pl.when(valid)
            def _():
                def wait_for(which):
                    if which == 0:
                        lat_copy(2, which, src_outer, 1 - inner).wait_recv()
                    else:
                        @pl.when((src_outer > 0) & (src_outer < outers - 1))
                        def _():
                            lat_copy(2, which, src_outer, 1 - inner).wait_recv()

                pair_rows(src_outer, wait_for)

            return carry

        lax.fori_loop(0, 2, pair, 0)

        @pl.when(step == outers - 1)
        def _():
            for which in range(2):
                for k in range(toks // 2 - 1, 0, -1):
                    held_copy(which, False, toks // 2 - k).wait_recv()
                    held_copy(which, True, k).start()

        @pl.when(step == outers - 2)
        def _():
            for k in range(toks):
                if k:
                    band_copy(k).wait_recv()
            for k in range(toks):
                xturned[:, k * rows:(k + 1) * rows] = jnp.transpose(xband[k])

        return carry

    lax.fori_loop(0, outers + 1, arrivals, 0)

    for k in range(1, lanes):
        peer = at_lane(k)
        pltpu.make_async_remote_copy(
            src_ref=gate_send.at[peer], dst_ref=gate_recv.at[peer],
            send_sem=gate_ss.at[peer], recv_sem=gate_rs.at[peer],
            device_id={"exp": peer}, device_id_type=MESH,
        ).wait_recv()
    gate_rows[...] = jnp.zeros_like(gate_rows)
    for e in range(window):
        gate_rows[tok, e:e + 1, :] = gate_recv[2 * e, 0:1, :] + gate_recv[2 * e + 1, 0:1, :]

    def row_copy(k):
        return pltpu.make_async_remote_copy(
            src_ref=gate_rows.at[tok, pl.ds(0, pad)], dst_ref=rows_recv.at[tok],
            send_sem=log_ss.at[k], recv_sem=log_rs.at[toks - k],
            device_id={"tok": at_tok(k)}, device_id_type=MESH,
        )

    for k in range(1, toks):
        row_copy(k).start()

    def logit_rows(t):
        head = held_all[1, t, :, :128] + jnp.transpose(gate_rows[t])
        gate_grad = jnp.concatenate([head, held_all[1, t, :, 128:]], axis=1)
        prob = held_all[0, t]
        centre = jnp.sum(prob * gate_grad, axis=1, keepdims=True)
        logits_all[t] = (prob * (gate_grad - centre)).astype(BF16)

    logit_rows(tok)

    terms = jnp.dot(
        packed[...].reshape(lanes * SLOTS, packed.shape[2]), win[...], preferred_element_type=F32
    )
    term_send[...] = terms.astype(BF16).reshape(term_send.shape)

    def term_copy(k):
        return pltpu.make_async_remote_copy(
            src_ref=term_send.at[at_lane(k)], dst_ref=term_recv.at[lane],
            send_sem=term_ss.at[k], recv_sem=term_rs.at[lanes - k],
            device_id={"exp": at_lane(k)}, device_id_type=MESH,
        )

    for k in range(1, lanes):
        term_copy(k).start()
    term_recv[lane] = term_send[lane]

    for which in range(2):
        for k in range(toks // 2):
            held_copy(which, True, k).wait_recv()
    for k in range(1, toks):
        peer = at_tok(k)
        pltpu.make_async_remote_copy(
            src_ref=gate_rows.at[tok, pl.ds(0, pad)], dst_ref=rows_recv.at[peer],
            send_sem=log_ss.at[k], recv_sem=log_rs.at[k],
            device_id={"tok": peer}, device_id_type=MESH,
        ).wait_recv()
        gate_rows[peer, :pad] = rows_recv[peer]
        logit_rows(peer)

    experts = rw.shape[1]
    band_logits = logits_all[...].reshape(toks * rows, experts)

    def part_block(d):
        span = 2 * own_rows
        part[d] = jnp.dot(
            xturned[pl.ds(pl.multiple_of(d * span, span), span)], band_logits, preferred_element_type=F32
        ).reshape(2, own_rows, experts)
        ax_send[d] = part[d, 1 - inner, :half].astype(BF16)
        ax_copy(d).start()

    neighbour = outer * 2 + 1 - inner

    def ax_copy(d):
        return pltpu.make_async_remote_copy(
            src_ref=ax_send.at[d], dst_ref=ax_recv.at[d], send_sem=ax_ss.at[d], recv_sem=ax_rs.at[d],
            device_id={"exp": neighbour}, device_id_type=MESH,
        )

    def line_copy(send, recv, ss, rs, way, side, d):
        return pltpu.make_async_remote_copy(
            src_ref=send.at[way, d], dst_ref=recv.at[way, d], send_sem=ss.at[way, d],
            recv_sem=rs.at[way, d], device_id={"exp": lane + 2 * side}, device_id_type=MESH,
        )

    def line_item(m):
        j, q = m // 2, m % 2
        side = (1 - 2 * ((outer * 2) // outers)) * (1 - 2 * q)
        d = ((side + 1) // 2) * (outers - 1 - 2 * j) + j
        return (1 - side) // 2, side, d

    def ax_start(m, carry):
        way, side, d = line_item(m)

        @pl.when((d - outer) * side > 0)
        def _():
            part_block(d)

        return carry

    lax.fori_loop(0, 2 * outers, ax_start, 0)
    part_block(outer)

    def ax_wait(d):
        ax_copy(d).wait_recv()
        part[d, inner, :half] = part[d, inner, :half] + ax_recv[d].astype(F32)

    def line(send, recv, ss, rs, own, ready):
        def item(m, carry):
            way, side, d = line_item(m)
            ahead = (d - outer) * side > 0
            behind = (outer - side >= 0) & (outer - side < outers)

            @pl.when(ahead)
            def _():
                ready(d)

            @pl.when(ahead & behind)
            def _():
                line_copy(send, recv, ss, rs, way, side, d).wait_recv()
                send[way, d] = (own(d) + recv[way, d].astype(F32)).astype(BF16)

            @pl.when(ahead & jnp.logical_not(behind))
            def _():
                send[way, d] = own(d).astype(BF16)

            @pl.when(ahead)
            def _():
                line_copy(send, recv, ss, rs, way, side, d).start()

            return carry

        lax.fori_loop(0, 2 * outers, item, 0)

    def line_end(send, recv, ss, rs, total):
        for way, side in ((0, 1), (1, -1)):
            @pl.when((outer - side >= 0) & (outer - side < outers))
            def _():
                line_copy(send, recv, ss, rs, way, side, outer).wait_recv()
                total[...] = total[...] + recv[way, outer].astype(F32)

    def line_sent(send, recv, ss, rs):
        def item(m, carry):
            way, side, d = line_item(m)

            @pl.when((d - outer) * side > 0)
            def _():
                line_copy(send, recv, ss, rs, way, side, d).wait_send()

            return carry

        lax.fori_loop(0, 2 * outers, item, 0)

    line_b = (bz_send, bz_recv, bz_ss, bz_rs)
    line_a = (az_send, az_recv, az_ss, az_rs)
    line(*line_b, lambda d: part[d, :, half:], lambda d: None)
    line(*line_a, lambda d: part[d, inner, :half], ax_wait)
    total_b[...] = part[outer, :, half:]
    line_end(*line_b, total_b)
    bx_send[...] = total_b[1 - inner].astype(BF16)
    bx = pltpu.make_async_remote_copy(
        src_ref=bx_send, dst_ref=bx_recv, send_sem=bx_ss, recv_sem=bx_rs,
        device_id={"exp": neighbour}, device_id_type=MESH,
    )
    bx.start()

    for k in range(1, lanes):
        peer = at_lane(k)
        pltpu.make_async_remote_copy(
            src_ref=term_send.at[peer], dst_ref=term_recv.at[peer],
            send_sem=term_ss.at[k], recv_sem=term_rs.at[k],
            device_id={"exp": peer}, device_id_type=MESH,
        ).wait_recv()
    own_hits = own_hits_ref[...]
    own_rank = jnp.dot(own_hits.astype(BF16), before, preferred_element_type=F32) - 1.0
    spread = []
    for e in range(window):
        block = ((own_hits[e:e + 1] > 0.0) & (own_rank[e:e + 1] == slot_iota)).astype(F32)
        spread += [block, block]
    spread = jnp.transpose(jnp.concatenate(spread, axis=0)).astype(BF16)
    latent_out[...] = jnp.dot(
        spread, term_recv[...].reshape(lanes * SLOTS, term_recv.shape[2]), preferred_element_type=F32
    ).astype(BF16)

    stores[0].start()
    xgrad_out[...] = lax.dot_general(logits_all[tok], rw[...], NT, preferred_element_type=F32).astype(BF16)
    stores[1].start()

    ax_wait(outer)
    total_a[...] = part[outer, inner, :half]
    line_end(*line_a, total_a)
    rwg_out[:half] = total_a[...]
    bx.wait_recv()
    rwg_out[half:] = total_b[inner] + bx_recv[...].astype(F32)

    for store in stores:
        store.wait()
    def sent(src_outer, carry):
        for which in range(2):
            forward(which, src_outer, lambda c: c.wait_send())
        chain(src_outer, lambda c: c.wait_send())
        return carry

    lax.fori_loop(0, outers, sent, 0)
    for k in range(1, lanes):
        pick_copy(k).wait_send()
        gate_copy(at_lane(k)).wait_send()
        term_copy(k).wait_send()
    for k in range(1, toks):
        band_copy(k).wait_send()
    for d in range(outers):
        ax_copy(d).wait_send()
    line_sent(*line_b)
    line_sent(*line_a)
    bx.wait_send()
    for k in range(1, toks):
        row_copy(k).wait_send()
    for which in range(2):
        for k in range(toks // 2):
            held_copy(which, True, k).wait_send()
            if k:
                held_copy(which, False, k).wait_send()


def hand_over(*refs):
    count = len(refs) // 3
    sems = refs[-1]
    ins, outs, held = refs[:count], refs[count:2 * count], refs[2 * count:3 * count]
    loads = [pltpu.make_async_copy(ins[k], held[k], sems.at[k]) for k in range(count)]
    stores = [pltpu.make_async_copy(held[k], outs[k], sems.at[count + k]) for k in range(count)]
    for load in loads:
        load.start()
    for load, store in zip(loads, stores):
        load.wait()
        store.start()
    for store in stores:
        store.wait()


def shards(
    x_tokens, router_weight, gate_rest, latent_in, latent_grad, expert_picks, expert_in, expert_out
):
    toks = lax.axis_size("tok")
    lanes = lax.axis_size("exp")
    rows, width = x_tokens.shape
    experts = router_weight.shape[1]
    window = experts - gate_rest.shape[1]
    latent, hidden = expert_in.shape[1:]
    feats = width // toks
    own_rows = feats // lanes
    outers = lanes // 2
    half = max(16, own_rows * 3 // 4 // 16 * 16)
    tail = own_rows - half
    pad = -(-window // 8) * 8
    vmem = pl.BlockSpec(memory_space=pltpu.VMEM)
    anywhere = pl.BlockSpec(memory_space=pl.ANY)
    dma = pltpu.SemaphoreType.DMA
    results = pl.pallas_call(
        functools.partial(kernel, toks, lanes, window),
        out_shape=(
            jax.ShapeDtypeStruct((rows, latent), BF16),
            jax.ShapeDtypeStruct((rows, width), BF16),
            jax.ShapeDtypeStruct((own_rows, experts), F32),
        ),
        in_specs=[anywhere] * 8,
        out_specs=(anywhere, anywhere, vmem),
        scratch_shapes=[
            pltpu.VMEM((rows, width), BF16),
            pltpu.VMEM(gate_rest.shape, F32),
            pltpu.VMEM((expert_picks.shape[1], expert_picks.shape[0]), jnp.int32),
            pltpu.VMEM((rows, latent), BF16),
            pltpu.VMEM((rows, width), BF16),
            pltpu.VMEM((width, experts), BF16),
            pltpu.VMEM((hidden, latent), BF16),
            pltpu.VMEM((hidden, latent), BF16),
            pltpu.VMEM((2, lanes, rows, latent), BF16),
            pltpu.VMEM((2, toks, rows, experts), F32),
            pltpu.VMEM((lanes, pad, rows), F32),
            pltpu.VMEM((pad, rows), F32),
            pltpu.VMEM((lanes, 8, rows), F32),
            pltpu.VMEM((lanes, 8, rows), F32),
            pltpu.VMEM((toks, 128, rows), F32),
            pltpu.VMEM((toks, pad, rows), F32),
            pltpu.VMEM((rows, experts), F32),
            pltpu.VMEM((lanes, rows), F32),
            pltpu.VMEM((pad, rows), F32),
            pltpu.VMEM((lanes, rows), F32),
            pltpu.VMEM((lanes, SLOTS, hidden), BF16),
            pltpu.VMEM((2 * rows, hidden), F32),
            pltpu.VMEM((lanes, SLOTS, latent), BF16),
            pltpu.VMEM((lanes, SLOTS, latent), BF16),
            pltpu.VMEM((toks, rows, feats), BF16),
            pltpu.VMEM((feats, toks * rows), BF16),
            pltpu.VMEM((toks, rows, experts), BF16),
            pltpu.VMEM((outers, 2, own_rows, experts), F32),
            pltpu.VMEM((outers, half, experts), BF16),
            pltpu.VMEM((outers, half, experts), BF16),
            pltpu.VMEM((2, outers, 2, tail, experts), BF16),
            pltpu.VMEM((2, outers, 2, tail, experts), BF16),
            pltpu.VMEM((tail, experts), BF16),
            pltpu.VMEM((tail, experts), BF16),
            pltpu.VMEM((2, outers, half, experts), BF16),
            pltpu.VMEM((2, outers, half, experts), BF16),
            pltpu.VMEM((half, experts), F32),
            pltpu.VMEM((2, tail, experts), F32),
            dma((10,)),
            dma((3, 2, outers)),
            dma((2,)),
            dma((2, outers)),
            dma((2, outers)),
            dma((lanes,)), dma((lanes,)),
            dma((lanes,)), dma((lanes,)),
            dma((lanes,)), dma((lanes,)),
            dma((toks,)), dma((toks,)),
            dma((toks,)), dma((toks,)),
            dma((2, toks)), dma((2, toks)),
            dma((outers,)), dma((outers,)),
            dma((2, outers)), dma((2, outers)),
            dma, dma,
            dma((2, outers)), dma((2, outers)),
        ],
        compiler_params=pltpu.CompilerParams(
            collective_id=0, has_side_effects=True, vmem_limit_bytes=56 * 1024 * 1024
        ),
    )(
        x_tokens, gate_rest, latent_in, latent_grad, expert_picks.T, router_weight,
        jnp.swapaxes(expert_in, 1, 2), expert_out,
    )
    return pl.pallas_call(
        hand_over,
        out_shape=tuple(jax.ShapeDtypeStruct(r.shape, r.dtype) for r in results),
        in_specs=[anywhere] * len(results),
        out_specs=(anywhere,) * len(results),
        scratch_shapes=[pltpu.VMEM(r.shape, r.dtype) for r in results] + [dma((2 * len(results),))],
    )(*results)


def solution(mesh):
    placed = (
        P(("tok", "exp"), None),
        P(),
        P(("tok", "exp"), None),
        P(("tok", "exp"), None),
        P(("tok", "exp"), None),
        P("tok", None),
        P("exp", None, None),
        P("exp", None, None),
    )
    return jax.shard_map(
        shards,
        mesh=mesh,
        in_specs=placed,
        out_specs=(P(("tok", "exp"), None), P(("tok", "exp"), None), P(("tok", "exp"), None)),
        check_vma=False,
    )
```

```python
import functools
import jax
import jax.numpy as jnp
from jax import lax
from jax.experimental import pallas as pl
from jax.experimental.pallas import tpu as pltpu
from jax.sharding import PartitionSpec as P

MESH = pl.DeviceIdType.MESH
F32 = jnp.float32
BF16 = jnp.bfloat16
NT = (((1,), (1,)), ((), ()))
SLOTS = 16


def kernel(
    toks, lanes, window,
    x_hbm, gate_hbm, latin_hbm, latgrad_hbm, picks_hbm, rw_hbm, win_hbm, wout_hbm,
    latent_hbm, xgrad_hbm, rwg_out,
    x_ref, gate_ref, picks_ref, latent_out, xgrad_out,
    rw, win, wout, lat, held_all, pick_recv, pick_send, gate_recv, gate_send, gate_rows, rows_recv, gate_grads, hits_ref, own_hits_ref, rank, packed, active_ref,
    term_send, term_recv, xband, xturned, logits_all, part, ax_send, ax_recv,
    bz_send, bz_recv, bx_send, bx_recv, az_send, az_recv, total_a, total_b,
    load_sem, send_lat, chain_ss, recv_z, recv_x, pick_ss, pick_rs, gate_ss, gate_rs, term_ss, term_rs,
    band_ss, band_rs, log_ss, log_rs, held_ss, held_rs, ax_ss, ax_rs, bz_ss, bz_rs, bx_ss, bx_rs,
    az_ss, az_rs,
):
    tok = lax.axis_index("tok")
    lane = lax.axis_index("exp")
    outers = lanes // 2
    outer = lane // 2
    inner = lane % 2
    expert = lane // 2
    rows = x_ref.shape[0]
    own_rows = rwg_out.shape[0]
    feats = x_ref.shape[1] // toks
    half = ax_send.shape[1]

    first_loads = [
        pltpu.make_async_copy(latin_hbm, lat.at[0, lane], load_sem.at[3]),
        pltpu.make_async_copy(latgrad_hbm, lat.at[1, lane], load_sem.at[4]),
        pltpu.make_async_copy(x_hbm, x_ref, load_sem.at[5]),
        pltpu.make_async_copy(picks_hbm, picks_ref, load_sem.at[6]),
        pltpu.make_async_copy(gate_hbm, gate_ref, load_sem.at[7]),
    ]
    loads = [
        pltpu.make_async_copy(rw_hbm, rw, load_sem.at[0]),
        pltpu.make_async_copy(win_hbm.at[0], win, load_sem.at[1]),
        pltpu.make_async_copy(wout_hbm.at[0], wout, load_sem.at[2]),
    ]
    stores = [
        pltpu.make_async_copy(latent_out, latent_hbm, load_sem.at[8]),
        pltpu.make_async_copy(xgrad_out, xgrad_hbm, load_sem.at[9]),
    ]
    for load in first_loads + loads:
        load.start()

    def at_lane(k):
        return lax.rem(lane + k, lanes)

    def at_tok(k):
        return lax.rem(tok + k, toks)

    barrier = pltpu.get_barrier_semaphore()
    for k in range(1, lanes):
        pl.semaphore_signal(barrier, inc=1, device_id={"exp": at_lane(k)}, device_id_type=MESH)
    for k in range(1, toks):
        pl.semaphore_signal(barrier, inc=1, device_id={"tok": at_tok(k)}, device_id_type=MESH)
    first_loads[0].wait()
    first_loads[1].wait()
    pl.semaphore_wait(barrier, lanes - 1 + toks - 1)

    def lat_copy(kind, which, src_outer, src_inner):
        slot = src_outer * 2 + src_inner
        if kind == 2:
            peer, recv = outer * 2 + 1 - inner, recv_x.at[which, src_outer]
        else:
            peer, recv = lane + (2 if kind == 0 else -2), recv_z.at[which, src_outer]
        return pltpu.make_async_remote_copy(
            src_ref=lat.at[which, slot], dst_ref=lat.at[which, slot],
            send_sem=send_lat.at[kind, which, src_outer], recv_sem=recv,
            device_id={"exp": peer}, device_id_type=MESH,
        )

    def forward(which, src_outer, do):
        @pl.when((src_outer <= outer) & (outer < outers - 1))
        def _():
            do(lat_copy(0, which, src_outer, inner))

        @pl.when((src_outer >= outer) & (outer > 0))
        def _():
            do(lat_copy(1, which, src_outer, inner))

        if which == 0:
            do(lat_copy(2, which, src_outer, inner))
        else:
            @pl.when((src_outer == outer) | ((src_outer > 0) & (src_outer < outers - 1)))
            def _():
                do(lat_copy(2, which, src_outer, inner))

    def chain(src_outer, do):
        slot = src_outer * 2 + 1 - inner
        for side, end in ((1, 0), (-1, outers - 1)):
            @pl.when((src_outer == end) & (outer + side >= 0) & (outer + side < outers))
            def _():
                do(pltpu.make_async_remote_copy(
                    src_ref=lat.at[1, slot], dst_ref=lat.at[1, slot],
                    send_sem=chain_ss.at[0 if side == 1 else 1], recv_sem=recv_x.at[1, src_outer],
                    device_id={"exp": lane + 2 * side}, device_id_type=MESH,
                ))

    for which in range(2):
        forward(which, outer, lambda c: c.start())

    def band_copy(k):
        peer = at_tok(k)
        return pltpu.make_async_remote_copy(
            src_ref=x_ref.at[:, pl.ds(pl.multiple_of(peer * feats, 128), feats)],
            dst_ref=xband.at[tok],
            send_sem=band_ss.at[k], recv_sem=band_rs.at[toks - k],
            device_id={"tok": peer}, device_id_type=MESH,
        )

    for load in first_loads[2:]:
        load.wait()
    for k in range(1, toks):
        band_copy(k).start()
    xband[tok] = x_ref[:, pl.ds(pl.multiple_of(tok * feats, 128), feats)]

    def any_row(picks, e):
        return jnp.max((picks == e).astype(F32), axis=0, keepdims=True)

    group_hits = any_row(picks_ref[...], expert)
    for k in range(lanes):
        hits_ref[k:k + 1, :] = group_hits[:, k * rows:(k + 1) * rows]
    own_picks = picks_ref[:, pl.ds(pl.multiple_of(lane * rows, rows), rows)]
    own_hits_ref[...] = jnp.zeros_like(own_hits_ref)
    for e in range(window):
        own_hits_ref[e:e + 1, :] = any_row(own_picks, e)
    rest = gate_ref.shape[1]
    gate_grads[:, rest - rest % 128:] = jnp.zeros_like(gate_grads[:, rest - rest % 128:])
    gate_grads[:, :rest] = gate_ref[...]
    held_all[1, tok] = pltpu.roll(gate_grads[...], window, 1)
    sibling = tok + 1 - 2 * lax.rem(tok, 2)

    def held_copy(which, to_sibling, k):
        far = lax.rem(tok + 2 * k, toks)
        src = far if to_sibling else tok
        sem = (toks // 2 + k) if to_sibling else (toks // 2 - k) % (toks // 2)
        return pltpu.make_async_remote_copy(
            src_ref=held_all.at[which, src], dst_ref=held_all.at[which, src],
            send_sem=held_ss.at[which, toks // 2 + k if to_sibling else k], recv_sem=held_rs.at[which, sem],
            device_id={"tok": sibling if to_sibling else far}, device_id_type=MESH,
        )

    def held_start(which):
        for k in range(1, toks // 2):
            held_copy(which, False, k).start()
        held_copy(which, True, 0).start()

    held_start(1)

    loads[0].wait()
    logits = jnp.dot(x_ref[...], rw[...], preferred_element_type=F32)
    shifted = jnp.exp(logits - jnp.max(logits, axis=1, keepdims=True))
    held_all[0, tok] = shifted / jnp.sum(shifted, axis=1, keepdims=True)
    pad = own_hits_ref.shape[0]
    pick_send[...] = jnp.transpose(held_all[0, tok, :, :128])[:pad] * own_hits_ref[...]
    pick_recv[0] = pick_send[...]

    def pick_copy(k):
        return pltpu.make_async_remote_copy(
            src_ref=pick_send, dst_ref=pick_recv.at[lanes - k],
            send_sem=pick_ss.at[k], recv_sem=pick_rs.at[lanes - k],
            device_id={"exp": at_lane(k)}, device_id_type=MESH,
        )

    for k in range(1, lanes):
        pick_copy(k).start()
    held_start(0)
    before = (
        lax.broadcasted_iota(jnp.int32, (rows, rows), 0)
        <= lax.broadcasted_iota(jnp.int32, (rows, rows), 1)
    ).astype(BF16)
    rank[...] = jnp.dot(hits_ref[...].astype(BF16), before, preferred_element_type=F32) - 1.0
    slot_iota = lax.broadcasted_iota(jnp.int32, (SLOTS, rows), 0).astype(F32)
    loads[1].wait()
    loads[2].wait()
    for k in range(1, lanes):
        pick_copy(k).wait_recv()

    def gate_copy(src_lane):
        return pltpu.make_async_remote_copy(
            src_ref=gate_send.at[src_lane], dst_ref=gate_recv.at[lane],
            send_sem=gate_ss.at[src_lane], recv_sem=gate_rs.at[lane],
            device_id={"exp": src_lane}, device_id_type=MESH,
        )

    def pair_rows(src_outer, wait_for):
        first = src_outer * 2
        both = lat.shape[3]
        wait_for(0)
        rows_in = lat[0, pl.ds(first, 2)].reshape(2 * rows, both)
        active_ref[...] = jnp.maximum(lax.dot_general(rows_in, win[...], NT, preferred_element_type=F32), 0.0)
        wait_for(1)
        rows_grad = lat[1, pl.ds(first, 2)].reshape(2 * rows, both)
        grad = lax.dot_general(rows_grad, wout[...], NT, preferred_element_type=F32)
        active = active_ref[...]
        product = active * grad
        gate = jnp.sum(active * product, axis=1, keepdims=True)
        gate_row = jnp.transpose(jnp.broadcast_to(gate, (2 * rows, 128)))[:8]
        for side in range(2):
            gate_send[first + side] = gate_row[:, side * rows:(side + 1) * rows]

            @pl.when(first + side == lane)
            def _():
                gate_recv[lane] = gate_row[:, side * rows:(side + 1) * rows]

            @pl.when(first + side != lane)
            def _():
                gate_copy(first + side).start()

        raw_rows = (2.0 * product).astype(BF16)
        for side in range(2):
            src_lane = first + side
            chosen = (
                (hits_ref[pl.ds(src_lane, 1), :] > 0.0) & (rank[pl.ds(src_lane, 1), :] == slot_iota)
            ).astype(F32)
            picked = pick_recv[lax.rem(src_lane - lane + lanes, lanes), pl.ds(expert, 1), :]
            scale = jnp.sum(chosen * picked, axis=1, keepdims=True)
            raw = jnp.dot(
                chosen.astype(BF16), raw_rows[side * rows:(side + 1) * rows], preferred_element_type=F32
            )
            packed[src_lane] = (raw * scale).astype(BF16)

    def arrivals(step, carry):
        for side in (-1, 1):
            src_outer = outer + side * step

            @pl.when((step > 0) & (step < outers) & (src_outer >= 0) & (src_outer < outers))
            def _():
                for which in range(2):
                    lat_copy(0, which, src_outer, inner).wait_recv()
                    forward(which, src_outer, lambda c: c.start())

        for side in (-1, 1):
            far = outer + side * (step - 1)

            @pl.when((step > 0) & ((step > 1) | (side == 1)) & ((far == 0) | (far == outers - 1)))
            def _():
                lat_copy(2, 1, far, 1 - inner).wait_recv()
                chain(far, lambda c: c.start())

        def pair(q, carry):
            distance = step - 1
            src_outer = outer + (2 * q - 1) * distance
            valid = (src_outer >= 0) & (src_outer < outers) & (distance >= 0)
            valid = valid & ((distance > 0) | (q == 0))

            @pl.when(valid)
            def _():
                def wait_for(which):
                    if which == 0:
                        lat_copy(2, which, src_outer, 1 - inner).wait_recv()
                    else:
                        @pl.when((src_outer > 0) & (src_outer < outers - 1))
                        def _():
                            lat_copy(2, which, src_outer, 1 - inner).wait_recv()

                pair_rows(src_outer, wait_for)

            return carry

        lax.fori_loop(0, 2, pair, 0)

        @pl.when(step == outers - 1)
        def _():
            for which in range(2):
                for k in range(toks // 2 - 1, 0, -1):
                    held_copy(which, False, toks // 2 - k).wait_recv()
                    held_copy(which, True, k).start()
            for k in range(toks):
                if k:
                    band_copy(k).wait_recv()
            for k in range(toks):
                xturned[:, k * rows:(k + 1) * rows] = jnp.transpose(xband[k])

        return carry

    lax.fori_loop(0, outers + 1, arrivals, 0)

    for k in range(1, lanes):
        peer = at_lane(k)
        pltpu.make_async_remote_copy(
            src_ref=gate_send.at[peer], dst_ref=gate_recv.at[peer],
            send_sem=gate_ss.at[peer], recv_sem=gate_rs.at[peer],
            device_id={"exp": peer}, device_id_type=MESH,
        ).wait_recv()
    gate_rows[...] = jnp.zeros_like(gate_rows)
    for e in range(window):
        gate_rows[tok, e:e + 1, :] = gate_recv[2 * e, 0:1, :] + gate_recv[2 * e + 1, 0:1, :]

    def row_copy(k):
        return pltpu.make_async_remote_copy(
            src_ref=gate_rows.at[tok, pl.ds(0, pad)], dst_ref=rows_recv.at[tok],
            send_sem=log_ss.at[k], recv_sem=log_rs.at[toks - k],
            device_id={"tok": at_tok(k)}, device_id_type=MESH,
        )

    for k in range(1, toks):
        row_copy(k).start()

    def logit_rows(t):
        head = held_all[1, t, :, :128] + jnp.transpose(gate_rows[t])
        gate_grad = jnp.concatenate([head, held_all[1, t, :, 128:]], axis=1)
        prob = held_all[0, t]
        centre = jnp.sum(prob * gate_grad, axis=1, keepdims=True)
        logits_all[t] = (prob * (gate_grad - centre)).astype(BF16)

    logit_rows(tok)

    terms = jnp.dot(
        packed[...].reshape(lanes * SLOTS, packed.shape[2]), win[...], preferred_element_type=F32
    )
    term_send[...] = terms.astype(BF16).reshape(term_send.shape)

    def term_copy(k):
        return pltpu.make_async_remote_copy(
            src_ref=term_send.at[at_lane(k)], dst_ref=term_recv.at[lane],
            send_sem=term_ss.at[k], recv_sem=term_rs.at[lanes - k],
            device_id={"exp": at_lane(k)}, device_id_type=MESH,
        )

    for k in range(1, lanes):
        term_copy(k).start()
    term_recv[lane] = term_send[lane]

    for which in range(2):
        for k in range(toks // 2):
            held_copy(which, True, k).wait_recv()
    for k in range(1, toks):
        peer = at_tok(k)
        pltpu.make_async_remote_copy(
            src_ref=gate_rows.at[tok, pl.ds(0, pad)], dst_ref=rows_recv.at[peer],
            send_sem=log_ss.at[k], recv_sem=log_rs.at[k],
            device_id={"tok": peer}, device_id_type=MESH,
        ).wait_recv()
        gate_rows[peer, :pad] = rows_recv[peer]
        logit_rows(peer)

    experts = rw.shape[1]
    part[...] = jnp.dot(
        xturned[...], logits_all[...].reshape(toks * rows, experts), preferred_element_type=F32
    ).reshape(part.shape)
    neighbour = outer * 2 + 1 - inner

    def ax_copy(d):
        return pltpu.make_async_remote_copy(
            src_ref=ax_send.at[d], dst_ref=ax_recv.at[d], send_sem=ax_ss.at[d], recv_sem=ax_rs.at[d],
            device_id={"exp": neighbour}, device_id_type=MESH,
        )

    def line_copy(send, recv, ss, rs, way, side, d):
        return pltpu.make_async_remote_copy(
            src_ref=send.at[way, d], dst_ref=recv.at[way, d], send_sem=ss.at[way, d],
            recv_sem=rs.at[way, d], device_id={"exp": lane + 2 * side}, device_id_type=MESH,
        )

    def line_item(m):
        j, q = m // 2, m % 2
        side = (1 - 2 * ((outer * 2) // outers)) * (1 - 2 * q)
        d = ((side + 1) // 2) * (outers - 1 - 2 * j) + j
        return (1 - side) // 2, side, d

    def ax_start(m, carry):
        way, side, d = line_item(m)

        @pl.when((d - outer) * side > 0)
        def _():
            ax_send[d] = part[d, 1 - inner, :half].astype(BF16)
            ax_copy(d).start()

        return carry

    lax.fori_loop(0, 2 * outers, ax_start, 0)
    ax_send[outer] = part[outer, 1 - inner, :half].astype(BF16)
    ax_copy(outer).start()

    def ax_wait(d):
        ax_copy(d).wait_recv()
        part[d, inner, :half] = part[d, inner, :half] + ax_recv[d].astype(F32)

    def line(send, recv, ss, rs, own, ready):
        def item(m, carry):
            way, side, d = line_item(m)
            ahead = (d - outer) * side > 0
            behind = (outer - side >= 0) & (outer - side < outers)

            @pl.when(ahead)
            def _():
                ready(d)

            @pl.when(ahead & behind)
            def _():
                line_copy(send, recv, ss, rs, way, side, d).wait_recv()
                send[way, d] = (own(d) + recv[way, d].astype(F32)).astype(BF16)

            @pl.when(ahead & jnp.logical_not(behind))
            def _():
                send[way, d] = own(d).astype(BF16)

            @pl.when(ahead)
            def _():
                line_copy(send, recv, ss, rs, way, side, d).start()

            return carry

        lax.fori_loop(0, 2 * outers, item, 0)

    def line_end(send, recv, ss, rs, total):
        for way, side in ((0, 1), (1, -1)):
            @pl.when((outer - side >= 0) & (outer - side < outers))
            def _():
                line_copy(send, recv, ss, rs, way, side, outer).wait_recv()
                total[...] = total[...] + recv[way, outer].astype(F32)

    def line_sent(send, recv, ss, rs):
        def item(m, carry):
            way, side, d = line_item(m)

            @pl.when((d - outer) * side > 0)
            def _():
                line_copy(send, recv, ss, rs, way, side, d).wait_send()

            return carry

        lax.fori_loop(0, 2 * outers, item, 0)

    line_b = (bz_send, bz_recv, bz_ss, bz_rs)
    line_a = (az_send, az_recv, az_ss, az_rs)
    line(*line_b, lambda d: part[d, :, half:], lambda d: None)
    line(*line_a, lambda d: part[d, inner, :half], ax_wait)
    total_b[...] = part[outer, :, half:]
    line_end(*line_b, total_b)
    bx_send[...] = total_b[1 - inner].astype(BF16)
    bx = pltpu.make_async_remote_copy(
        src_ref=bx_send, dst_ref=bx_recv, send_sem=bx_ss, recv_sem=bx_rs,
        device_id={"exp": neighbour}, device_id_type=MESH,
    )
    bx.start()

    for k in range(1, lanes):
        peer = at_lane(k)
        pltpu.make_async_remote_copy(
            src_ref=term_send.at[peer], dst_ref=term_recv.at[peer],
            send_sem=term_ss.at[k], recv_sem=term_rs.at[k],
            device_id={"exp": peer}, device_id_type=MESH,
        ).wait_recv()
    own_hits = own_hits_ref[...]
    own_rank = jnp.dot(own_hits.astype(BF16), before, preferred_element_type=F32) - 1.0
    spread = []
    for e in range(window):
        block = ((own_hits[e:e + 1] > 0.0) & (own_rank[e:e + 1] == slot_iota)).astype(F32)
        spread += [block, block]
    spread = jnp.transpose(jnp.concatenate(spread, axis=0)).astype(BF16)
    latent_out[...] = jnp.dot(
        spread, term_recv[...].reshape(lanes * SLOTS, term_recv.shape[2]), preferred_element_type=F32
    ).astype(BF16)

    stores[0].start()
    xgrad_out[...] = lax.dot_general(logits_all[tok], rw[...], NT, preferred_element_type=F32).astype(BF16)
    stores[1].start()

    ax_wait(outer)
    total_a[...] = part[outer, inner, :half]
    line_end(*line_a, total_a)
    rwg_out[:half] = total_a[...]
    bx.wait_recv()
    rwg_out[half:] = total_b[inner] + bx_recv[...].astype(F32)

    for store in stores:
        store.wait()
    def sent(src_outer, carry):
        for which in range(2):
            forward(which, src_outer, lambda c: c.wait_send())
        chain(src_outer, lambda c: c.wait_send())
        return carry

    lax.fori_loop(0, outers, sent, 0)
    for k in range(1, lanes):
        pick_copy(k).wait_send()
        gate_copy(at_lane(k)).wait_send()
        term_copy(k).wait_send()
    for k in range(1, toks):
        band_copy(k).wait_send()
    for d in range(outers):
        ax_copy(d).wait_send()
    line_sent(*line_b)
    line_sent(*line_a)
    bx.wait_send()
    for k in range(1, toks):
        row_copy(k).wait_send()
    for which in range(2):
        for k in range(toks // 2):
            held_copy(which, True, k).wait_send()
            if k:
                held_copy(which, False, k).wait_send()


def hand_over(*refs):
    count = len(refs) // 3
    sems = refs[-1]
    ins, outs, held = refs[:count], refs[count:2 * count], refs[2 * count:3 * count]
    loads = [pltpu.make_async_copy(ins[k], held[k], sems.at[k]) for k in range(count)]
    stores = [pltpu.make_async_copy(held[k], outs[k], sems.at[count + k]) for k in range(count)]
    for load in loads:
        load.start()
    for load, store in zip(loads, stores):
        load.wait()
        store.start()
    for store in stores:
        store.wait()


def shards(
    x_tokens, router_weight, gate_rest, latent_in, latent_grad, expert_picks, expert_in, expert_out
):
    toks = lax.axis_size("tok")
    lanes = lax.axis_size("exp")
    rows, width = x_tokens.shape
    experts = router_weight.shape[1]
    window = experts - gate_rest.shape[1]
    latent, hidden = expert_in.shape[1:]
    feats = width // toks
    own_rows = feats // lanes
    outers = lanes // 2
    half = max(16, own_rows * 7 // 8 // 16 * 16)
    tail = own_rows - half
    pad = -(-window // 8) * 8
    vmem = pl.BlockSpec(memory_space=pltpu.VMEM)
    anywhere = pl.BlockSpec(memory_space=pl.ANY)
    dma = pltpu.SemaphoreType.DMA
    results = pl.pallas_call(
        functools.partial(kernel, toks, lanes, window),
        out_shape=(
            jax.ShapeDtypeStruct((rows, latent), BF16),
            jax.ShapeDtypeStruct((rows, width), BF16),
            jax.ShapeDtypeStruct((own_rows, experts), F32),
        ),
        in_specs=[anywhere] * 8,
        out_specs=(anywhere, anywhere, vmem),
        scratch_shapes=[
            pltpu.VMEM((rows, width), BF16),
            pltpu.VMEM(gate_rest.shape, F32),
            pltpu.VMEM((expert_picks.shape[1], expert_picks.shape[0]), jnp.int32),
            pltpu.VMEM((rows, latent), BF16),
            pltpu.VMEM((rows, width), BF16),
            pltpu.VMEM((width, experts), BF16),
            pltpu.VMEM((hidden, latent), BF16),
            pltpu.VMEM((hidden, latent), BF16),
            pltpu.VMEM((2, lanes, rows, latent), BF16),
            pltpu.VMEM((2, toks, rows, experts), F32),
            pltpu.VMEM((lanes, pad, rows), F32),
            pltpu.VMEM((pad, rows), F32),
            pltpu.VMEM((lanes, 8, rows), F32),
            pltpu.VMEM((lanes, 8, rows), F32),
            pltpu.VMEM((toks, 128, rows), F32),
            pltpu.VMEM((toks, pad, rows), F32),
            pltpu.VMEM((rows, experts), F32),
            pltpu.VMEM((lanes, rows), F32),
            pltpu.VMEM((pad, rows), F32),
            pltpu.VMEM((lanes, rows), F32),
            pltpu.VMEM((lanes, SLOTS, hidden), BF16),
            pltpu.VMEM((2 * rows, hidden), F32),
            pltpu.VMEM((lanes, SLOTS, latent), BF16),
            pltpu.VMEM((lanes, SLOTS, latent), BF16),
            pltpu.VMEM((toks, rows, feats), BF16),
            pltpu.VMEM((feats, toks * rows), BF16),
            pltpu.VMEM((toks, rows, experts), BF16),
            pltpu.VMEM((outers, 2, own_rows, experts), F32),
            pltpu.VMEM((outers, half, experts), BF16),
            pltpu.VMEM((outers, half, experts), BF16),
            pltpu.VMEM((2, outers, 2, tail, experts), BF16),
            pltpu.VMEM((2, outers, 2, tail, experts), BF16),
            pltpu.VMEM((tail, experts), BF16),
            pltpu.VMEM((tail, experts), BF16),
            pltpu.VMEM((2, outers, half, experts), BF16),
            pltpu.VMEM((2, outers, half, experts), BF16),
            pltpu.VMEM((half, experts), F32),
            pltpu.VMEM((2, tail, experts), F32),
            dma((10,)),
            dma((3, 2, outers)),
            dma((2,)),
            dma((2, outers)),
            dma((2, outers)),
            dma((lanes,)), dma((lanes,)),
            dma((lanes,)), dma((lanes,)),
            dma((lanes,)), dma((lanes,)),
            dma((toks,)), dma((toks,)),
            dma((toks,)), dma((toks,)),
            dma((2, toks)), dma((2, toks)),
            dma((outers,)), dma((outers,)),
            dma((2, outers)), dma((2, outers)),
            dma, dma,
            dma((2, outers)), dma((2, outers)),
        ],
        compiler_params=pltpu.CompilerParams(
            collective_id=0, has_side_effects=True, vmem_limit_bytes=56 * 1024 * 1024
        ),
    )(
        x_tokens, gate_rest, latent_in, latent_grad, expert_picks.T, router_weight,
        jnp.swapaxes(expert_in, 1, 2), expert_out,
    )
    return pl.pallas_call(
        hand_over,
        out_shape=tuple(jax.ShapeDtypeStruct(r.shape, r.dtype) for r in results),
        in_specs=[anywhere] * len(results),
        out_specs=(anywhere,) * len(results),
        scratch_shapes=[pltpu.VMEM(r.shape, r.dtype) for r in results] + [dma((2 * len(results),))],
    )(*results)


def solution(mesh):
    placed = (
        P(("tok", "exp"), None),
        P(),
        P(("tok", "exp"), None),
        P(("tok", "exp"), None),
        P(("tok", "exp"), None),
        P("tok", None),
        P("exp", None, None),
        P("exp", None, None),
    )
    return jax.shard_map(
        shards,
        mesh=mesh,
        in_specs=placed,
        out_specs=(P(("tok", "exp"), None), P(("tok", "exp"), None), P(("tok", "exp"), None)),
        check_vma=False,
    )
```
